32 devices in a mesh: outer: 8 (over z, x), inner: 4 (over y, core).
Axes of the slice: x: 2, y: 2, z: 4, core: 2. Of those that a mesh axis runs over, the one named last changes fastest.
Arguments:
- query: bfloat16 [4096, 32, 128], P(('outer', 'inner')), may hold values from -6 to 6
- keys: bfloat16 [4096, 32, 128], P(('outer', 'inner')), may hold values from -6 to 6
- value: bfloat16 [4096, 32, 128], P(('outer', 'inner')), may hold values from -6 to 6
- beta: bfloat16 [4096, 32], P(('outer', 'inner')), may hold values from 0 to 1, as said below
Outputs:
- mixed: bfloat16 [4096, 32, 128], P(('outer', 'inner'))
The draws below stay inside these ranges and needn't reach their ends.
Inputs may be any that keep to these rules, and one draw needn't show every extreme that they name: `beta`: each gate lies strictly between 0 and 1.
All inputs are finite; a program needn't handle non-finite values.
Results may differ from the reference program's by a relative error of at most 0.001.
Values may be sent and summed in bfloat16 or wider, within the bound.
A program may use at most 128 MiB of HBM per device.

```python
import jax
import jax.numpy as jnp
from jax import lax

H = 32
DK = 128
SPAN = 128
SEQUENCE_TOKENS = 4096


def draw_beta(key, part):
    first, second, third, fourth, fifth_operand = jax.random.split(key, 5)
    slow_share = 0.5
    slow_head = jax.random.uniform(first, (H,)) < slow_share
    slow_rate = jax.random.uniform(second, (H,), minval=0.2, maxval=1.0) * (2.3 * DK / SEQUENCE_TOKENS)
    fast_rate = jax.random.uniform(third, (H,), minval=0.3, maxval=0.9)
    base = jnp.where(slow_head, slow_rate, fast_rate)
    factor = jnp.exp(jax.random.uniform(fourth, (SEQUENCE_TOKENS, H), minval=-0.7, maxval=0.7))
    gate_values = jnp.minimum(base[None, :] * factor, 0.98)
    token_span_block = jax.random.uniform(fifth_operand, (SEQUENCE_TOKENS, 1)) < 8.0 / SEQUENCE_TOKENS
    gate_values = jnp.where(token_span_block, 0.95, gate_values)
    return gate_values.astype(jnp.float32).astype(jnp.bfloat16)


def head_order(head_key):
    return jax.random.permutation(head_key, DK)


def draw_keys(key, part):
    values_key = jax.random.fold_in(key, 11)
    dims_key = jax.random.fold_in(key, 23)
    raw_values = jax.random.truncated_normal(values_key, -6.0, 6.0, (SEQUENCE_TOKENS, H, DK))
    ranked = jax.vmap(head_order)(jax.random.split(dims_key, H))
    weak_dims = ranked < DK // 8
    scaling = jnp.where(weak_dims, 0.05, 1.0).astype(jnp.float32)
    return (raw_values.astype(jnp.float32) * scaling[None, :, :]).astype(jnp.bfloat16)


def shard_levels(stream_key, shape, cuts, least, top_value):
    gain, own = 1.0, jax.random.fold_in(stream_key, 6)
    for axis_at, blocks in cuts:
        draws = jnp.exp(jax.random.uniform(jax.random.fold_in(own, axis_at), (blocks,), jnp.float32, least / len(cuts), top_value / len(cuts)))
        gain = gain * jnp.repeat(draws, shape[axis_at] // blocks).reshape([-1 if axis == axis_at else 1 for axis in range(len(shape))])
    return gain


def gaussian(rng, shape, spread, most, cuts=(), kind=jnp.bfloat16):
    values = spread * jax.random.normal(rng, shape, jnp.float32)
    if cuts:
        values = values * shard_levels(rng, shape, cuts, -0.22, 0.18)
    return jnp.clip(values, -most, most).astype(kind)


def setup_inputs(seed: int = 0) -> dict:
    key_of = jax.random.split(jax.random.key(seed), 5)
    query = gaussian(key_of[0], (SEQUENCE_TOKENS, H, DK), 1.0, 6.0, ((0, 32),))
    keys = draw_keys(jax.random.fold_in(key_of[4], 71), 0)
    value = gaussian(key_of[2], (SEQUENCE_TOKENS, H, DK), 1.0, 6.0, ((0, 32),))
    beta = draw_beta(jax.random.fold_in(key_of[4], 71), 0)
    return {"query": query, "keys": keys, "value": value, "beta": beta}


HIGH = lax.Precision.HIGHEST

def unit_rows(block):
    return block * lax.rsqrt(lax.optimization_barrier(jnp.sum(block * block, axis=-1, keepdims=True)) + 1e-06)

def span_terms(query_block, keys_c, value_c, beta_c):
    size = keys_c.shape[0]
    width = keys_c.shape[1]
    qnorm = unit_rows(query_block)
    knorm = unit_rows(keys_c)
    kbeta = knorm * beta_c[:, None]
    vbeta = value_c * beta_c[:, None]
    gram = jnp.dot(kbeta, knorm.T, precision=HIGH)
    lower = jnp.tril(gram, -1) + jnp.eye(size, dtype=jnp.float32)
    solved = jax.scipy.linalg.solve_triangular(lower, jnp.concatenate([kbeta, vbeta], axis=1), lower=True)
    weights = solved[:, :width]
    updates = solved[:, width:]
    scores = jnp.tril(jnp.dot(qnorm, knorm.T, precision=HIGH))
    return (qnorm, knorm, weights, updates, scores)

def reference(query, keys, value, beta):
    count = SEQUENCE_TOKENS // SPAN

    def blocks(array):
        return jnp.swapaxes(array.reshape(count, SPAN, H, DK), 1, 2)
    qblk = blocks(query)
    kblk = blocks(keys)
    vblk = blocks(value)
    bblk = jnp.swapaxes(beta.reshape(count, SPAN, H), 1, 2)
    terms_fn = jax.vmap(span_terms)

    def advance(state, inputs):
        qpart, kpart, vpart, bpart = inputs
        qnorm, knorm, weights, updates, scores = terms_fn(qpart.astype(jnp.float32), kpart.astype(jnp.float32), vpart.astype(jnp.float32), bpart.astype(jnp.float32))
        delta = updates - jnp.einsum('hcd,hde->hce', weights, state, precision=HIGH)
        result = jnp.einsum('hcd,hde->hce', qnorm, state, precision=HIGH) + jnp.einsum('hcs,hse->hce', scores, delta, precision=HIGH)
        state = state + jnp.einsum('hcd,hce->hde', knorm, delta, precision=HIGH)
        return (state, result.astype(jnp.bfloat16))
    start = jnp.zeros((H, DK, DK), jnp.float32)
    _, outputs = lax.scan(advance, start, (qblk, kblk, vblk, bblk))
    return jnp.swapaxes(outputs, 1, 2).reshape(SEQUENCE_TOKENS, H, DK)
```

```python
import functools

import jax
import jax.numpy as jnp
from jax import lax
from jax.experimental import pallas as pl
from jax.experimental.pallas import tpu as pltpu
from jax.sharding import PartitionSpec as P

SPAN = 128
GROUP = 4
F32 = jnp.float32
BF16 = jnp.bfloat16


def halves(x):
    high = x.astype(BF16)
    return high, (x - high.astype(F32)).astype(BF16)


def dot(a, b):
    return jnp.dot(a, b, preferred_element_type=F32)


def dot_halves(a, b):
    (ah, al), (bh, bl) = a, b
    return dot(jnp.concatenate([ah, al], 1), jnp.concatenate([bh, bh], 0)) + dot(ah, bl)


def dot_exact(a, b):
    ah, al = a
    return dot(jnp.concatenate([ah, al], 1), jnp.concatenate([b, b], 0))


def local_terms(query, keys, value, brow, rows, cols):
    eye = rows == cols
    both = lax.dot_general(
        jnp.concatenate([keys, query], 0), keys, (((1,), (1,)), ((), ())), preferred_element_type=F32
    )
    gram, raw = both[:SPAN], both[SPAN:]
    kf, qf = keys.astype(F32), query.astype(F32)
    diagonal = jnp.where(eye, gram, 0.0)
    krow = lax.rsqrt(jnp.sum(diagonal, axis=0, keepdims=True) + 1e-6)
    kcol = lax.rsqrt(jnp.sum(kf * kf, axis=1, keepdims=True) + 1e-6)
    qcol = lax.rsqrt(jnp.sum(qf * qf, axis=1, keepdims=True) + 1e-6)
    bcol = jnp.sum(jnp.where(eye, brow, 0.0), axis=1, keepdims=True)
    lower = jnp.where(rows > cols, gram * (bcol * kcol) * krow, 0.0)
    lh, ll = halves(lower)

    def merge_mask(level):
        return ((rows >> (level + 1)) == (cols >> (level + 1))) & (((rows >> level) & 1) == 1) & (((cols >> level) & 1) == 0)

    inverse = jnp.where(eye, 1.0, 0.0) - jnp.where(merge_mask(0), lower, 0.0)
    zero = jnp.zeros((), BF16)
    for level in range(1, (SPAN - 1).bit_length()):
        mask = merge_mask(level)
        part = (jnp.where(mask, lh, zero), jnp.where(mask, ll, zero))
        inv = halves(inverse)
        inverse = inverse - dot_halves(inv, halves(dot_halves(part, inv)))
    weights = dot_exact(halves(inverse * (brow * krow)), keys)
    updates = dot_exact(halves(inverse * brow), value)
    solved = jnp.concatenate([weights, updates], 1)
    scores = jnp.where(rows >= cols, raw * qcol * krow, 0.0)
    seen = dot_halves(halves(scores), halves(solved))
    nh, nl = halves(solved * kcol)
    written = lax.dot_general(
        jnp.concatenate([keys, keys], 0),
        jnp.concatenate([nh, nl], 0),
        (((0,), (0,)), ((), ())),
        preferred_element_type=F32,
    )
    width = keys.shape[1]
    trans = jnp.where(eye, 1.0, 0.0) - written[:, :width]
    reads = qf * qcol - seen[:, :width]
    return trans, written[:, width:], reads, seen[:, width:]


def kernel(outer, inner, q_ref, k_ref, v_ref, b_ref, o_ref, trans, offset, reads, local, came, goes, send_sem, recv_sem):
    heads = q_ref.shape[0]
    groups = heads // GROUP
    total = outer * inner
    me = lax.axis_index("outer") * inner + lax.axis_index("inner")
    after, before = lax.rem(me + 1, total), lax.rem(me + total - 1, total)

    def place(index):
        return (index // inner, lax.rem(index, inner))

    barrier = pltpu.get_barrier_semaphore()
    for other in (after, before):
        pl.semaphore_signal(barrier, inc=1, device_id=place(other), device_id_type=pl.DeviceIdType.MESH)
    pl.semaphore_wait(barrier, 2)

    def hop(h):
        return pltpu.make_async_remote_copy(
            src_ref=goes.at[h],
            dst_ref=came.at[h],
            send_sem=send_sem.at[h],
            recv_sem=recv_sem.at[h],
            device_id=place(after),
            device_id_type=pl.DeviceIdType.MESH,
        )

    @pl.when(me == 0)
    def _():
        came[...] = jnp.zeros_like(came)

    def prepare(g):
        rows = lax.broadcasted_iota(jnp.int32, (SPAN, SPAN), 0)
        cols = lax.broadcasted_iota(jnp.int32, (SPAN, SPAN), 1)
        for j in range(GROUP):
            h = g * GROUP + j
            a, b, p, o = local_terms(q_ref[h], k_ref[h], v_ref[h], b_ref[h], rows, cols)
            trans[h] = jnp.concatenate(halves(a), 1)
            offset[h] = b
            reads[h] = jnp.concatenate(halves(p), 1)
            local[h] = o

    def pass_on(g):
        for j in range(GROUP):
            h = g * GROUP + j

            @pl.when(me > 0)
            def _():
                hop(h).wait_recv()

            sh, sl = halves(came[h])
            a = trans[h]
            goes[h] = offset[h] + dot(a, jnp.concatenate([sh, sh], 0)) + dot(a[:, :SPAN], sl)

            @pl.when(me < total - 1)
            def _():
                hop(h).start()

        for j in range(GROUP):
            h = g * GROUP + j
            sh, sl = halves(came[h])
            p = reads[h]
            mixed = local[h] + dot(p, jnp.concatenate([sh, sh], 0)) + dot(p[:, :SPAN], sl)
            o_ref[h] = mixed.astype(BF16)

    ahead = jnp.minimum(groups, me // 2)

    def step(i, carry):
        @pl.when(i < groups)
        def _():
            prepare(i)

        @pl.when(i >= ahead)
        def _():
            pass_on(i - ahead)

        return carry

    lax.fori_loop(0, groups + ahead, step, 0)

    @pl.when(me < total - 1)
    def _():
        def drain(h, carry):
            hop(h).wait_send()
            return carry

        lax.fori_loop(0, heads, drain, 0)


def shards(outer, inner, query, keys, value, beta):
    tokens, heads, width = query.shape
    major = [jnp.transpose(x, (1, 0, 2)) for x in (query, keys, value)]
    gates = jnp.transpose(beta.astype(F32), (1, 0)).reshape(heads, 1, tokens)
    vmem = pl.BlockSpec(memory_space=pltpu.VMEM)
    mixed = pl.pallas_call(
        functools.partial(kernel, outer, inner),
        out_shape=jax.ShapeDtypeStruct((heads, tokens, width), BF16),
        in_specs=[vmem] * 4,
        out_specs=vmem,
        scratch_shapes=[
            pltpu.VMEM((heads, width, 2 * width), BF16),
            pltpu.VMEM((heads, width, width), F32),
            pltpu.VMEM((heads, tokens, 2 * width), BF16),
            pltpu.VMEM((heads, tokens, width), F32),
            pltpu.VMEM((heads, width, width), F32),
            pltpu.VMEM((heads, width, width), F32),
            pltpu.SemaphoreType.DMA((heads,)),
            pltpu.SemaphoreType.DMA((heads,)),
        ],
        compiler_params=pltpu.CompilerParams(
            collective_id=0, has_side_effects=True, vmem_limit_bytes=40 * 2**20
        ),
        cost_estimate=pl.CostEstimate(flops=heads * 60 * 2 * 128**3, bytes_accessed=2**22, transcendentals=0),
    )(*major, gates)
    return jnp.transpose(mixed, (1, 0, 2))


def solution(mesh):
    placed = P(("outer", "inner"), None, None)
    return jax.shard_map(
        functools.partial(shards, mesh.shape["outer"], mesh.shape["inner"]),
        mesh=mesh,
        in_specs=(placed, placed, placed, P(("outer", "inner"), None)),
        out_specs=placed,
        check_vma=False,
    )
```

```python
import functools

import jax
import jax.numpy as jnp
from jax import lax
from jax.experimental import pallas as pl
from jax.experimental.pallas import tpu as pltpu
from jax.sharding import PartitionSpec as P

SPAN = 128
GROUP = 4
F32 = jnp.float32
BF16 = jnp.bfloat16


def halves(x):
    high = x.astype(BF16)
    return high, (x - high.astype(F32)).astype(BF16)


def dot(a, b):
    return jnp.dot(a, b, preferred_element_type=F32)


def dot_halves(a, b):
    (ah, al), (bh, bl) = a, b
    return dot(jnp.concatenate([ah, al], 1), jnp.concatenate([bh, bh], 0)) + dot(ah, bl)


def dot_exact(a, b):
    ah, al = a
    return dot(jnp.concatenate([ah, al], 1), jnp.concatenate([b, b], 0))


def local_terms(query, keys, value, brow, rows, cols):
    eye = rows == cols
    width = keys[0].shape[1]
    count = range(len(keys))
    both = [
        lax.dot_general(
            jnp.concatenate([keys[i], query[i]], 0), keys[i], (((1,), (1,)), ((), ())), preferred_element_type=F32
        )
        for i in count
    ]
    gram, raw = [x[:SPAN] for x in both], [x[SPAN:] for x in both]
    kf, qf = [x.astype(F32) for x in keys], [x.astype(F32) for x in query]
    krow = [lax.rsqrt(jnp.sum(jnp.where(eye, x, 0.0), axis=0, keepdims=True) + 1e-6) for x in gram]
    kcol = [lax.rsqrt(jnp.sum(x * x, axis=1, keepdims=True) + 1e-6) for x in kf]
    qcol = [lax.rsqrt(jnp.sum(x * x, axis=1, keepdims=True) + 1e-6) for x in qf]
    bcol = [jnp.sum(jnp.where(eye, x, 0.0), axis=1, keepdims=True) for x in brow]
    lower = [jnp.where(rows > cols, gram[i] * (bcol[i] * kcol[i]) * krow[i], 0.0) for i in count]
    split = [halves(x) for x in lower]

    def merge_mask(level):
        return ((rows >> (level + 1)) == (cols >> (level + 1))) & (((rows >> level) & 1) == 1) & (((cols >> level) & 1) == 0)

    first = merge_mask(0)
    inverse = [jnp.where(eye, 1.0, 0.0) - jnp.where(first, x, 0.0) for x in lower]
    zero = jnp.zeros((), BF16)
    for level in range(1, (SPAN - 1).bit_length()):
        mask = merge_mask(level)
        part = [(jnp.where(mask, h, zero), jnp.where(mask, l, zero)) for h, l in split]
        inv = [halves(x) for x in inverse]
        inner = [dot_halves(part[i], inv[i]) for i in count]
        inner = [halves(x) for x in inner]
        change = [dot_halves(inv[i], inner[i]) for i in count]
        inverse = [inverse[i] - change[i] for i in count]
    for_keys = [halves(inverse[i] * (brow[i] * krow[i])) for i in count]
    for_value = [halves(inverse[i] * brow[i]) for i in count]
    weights = [dot_exact(for_keys[i], keys[i]) for i in count]
    updates = [dot_exact(for_value[i], value[i]) for i in count]
    solved = [jnp.concatenate([weights[i], updates[i]], 1) for i in count]
    scores = [jnp.where(rows >= cols, raw[i] * qcol[i] * krow[i], 0.0) for i in count]
    scaled = [halves(solved[i] * kcol[i]) for i in count]
    written = [
        lax.dot_general(
            jnp.concatenate([keys[i], keys[i]], 0),
            jnp.concatenate(scaled[i], 0),
            (((0,), (0,)), ((), ())),
            preferred_element_type=F32,
        )
        for i in count
    ]
    scores = [halves(x) for x in scores]
    solved = [halves(x) for x in solved]
    seen = [dot_halves(scores[i], solved[i]) for i in count]
    trans = [jnp.where(eye, 1.0, 0.0) - x[:, :width] for x in written]
    reads = [qf[i] * qcol[i] - seen[i][:, :width] for i in count]
    return trans, [x[:, width:] for x in written], reads, [x[:, width:] for x in seen]


def kernel(outer, inner, q_ref, k_ref, v_ref, b_ref, o_ref, trans, offset, reads, local, came, goes, send_sem, recv_sem):
    heads = q_ref.shape[0]
    groups = heads // GROUP
    total = outer * inner
    me = lax.axis_index("outer") * inner + lax.axis_index("inner")
    after, before = lax.rem(me + 1, total), lax.rem(me + total - 1, total)

    def place(index):
        return (index // inner, lax.rem(index, inner))

    barrier = pltpu.get_barrier_semaphore()
    for other in (after, before):
        pl.semaphore_signal(barrier, inc=1, device_id=place(other), device_id_type=pl.DeviceIdType.MESH)
    pl.semaphore_wait(barrier, 2)

    def hop(h):
        return pltpu.make_async_remote_copy(
            src_ref=goes.at[h],
            dst_ref=came.at[h],
            send_sem=send_sem.at[h],
            recv_sem=recv_sem.at[h],
            device_id=place(after),
            device_id_type=pl.DeviceIdType.MESH,
        )

    @pl.when(me == 0)
    def _():
        came[...] = jnp.zeros_like(came)

    def prepare(g):
        rows = lax.broadcasted_iota(jnp.int32, (SPAN, SPAN), 0)
        cols = lax.broadcasted_iota(jnp.int32, (SPAN, SPAN), 1)
        hs = [g * GROUP + j for j in range(GROUP)]
        found = local_terms(*([ref[h] for h in hs] for ref in (q_ref, k_ref, v_ref, b_ref)), rows, cols)
        for h, a, b, p, o in zip(hs, *found):
            trans[h] = jnp.concatenate(halves(a), 1)
            offset[h] = b
            reads[h] = jnp.concatenate(halves(p), 1)
            local[h] = o

    def pass_on(g):
        for j in range(GROUP):
            h = g * GROUP + j

            @pl.when(me > 0)
            def _():
                hop(h).wait_recv()

            sh, sl = halves(came[h])
            a = trans[h]
            goes[h] = offset[h] + dot(a, jnp.concatenate([sh, sh], 0)) + dot(a[:, :SPAN], sl)

            @pl.when(me < total - 1)
            def _():
                hop(h).start()

        for j in range(GROUP):
            h = g * GROUP + j
            sh, sl = halves(came[h])
            p = reads[h]
            mixed = local[h] + dot(p, jnp.concatenate([sh, sh], 0)) + dot(p[:, :SPAN], sl)
            o_ref[h] = mixed.astype(BF16)

    ahead = jnp.minimum(groups, 3 * me // 4)

    def step(i, carry):
        @pl.when(i < groups)
        def _():
            prepare(i)

        @pl.when(i >= ahead)
        def _():
            pass_on(i - ahead)

        return carry

    lax.fori_loop(0, groups + ahead, step, 0)

    @pl.when(me < total - 1)
    def _():
        def drain(h, carry):
            hop(h).wait_send()
            return carry

        lax.fori_loop(0, heads, drain, 0)


def shards(outer, inner, query, keys, value, beta):
    tokens, heads, width = query.shape
    major = [jnp.transpose(x, (1, 0, 2)) for x in (query, keys, value)]
    gates = jnp.transpose(beta.astype(F32), (1, 0)).reshape(heads, 1, tokens)
    vmem = pl.BlockSpec(memory_space=pltpu.VMEM)
    mixed = pl.pallas_call(
        functools.partial(kernel, outer, inner),
        out_shape=jax.ShapeDtypeStruct((heads, tokens, width), BF16),
        in_specs=[vmem] * 4,
        out_specs=vmem,
        scratch_shapes=[
            pltpu.VMEM((heads, width, 2 * width), BF16),
            pltpu.VMEM((heads, width, width), F32),
            pltpu.VMEM((heads, tokens, 2 * width), BF16),
            pltpu.VMEM((heads, tokens, width), F32),
            pltpu.VMEM((heads, width, width), F32),
            pltpu.VMEM((heads, width, width), F32),
            pltpu.SemaphoreType.DMA((heads,)),
            pltpu.SemaphoreType.DMA((heads,)),
        ],
        compiler_params=pltpu.CompilerParams(
            collective_id=0, has_side_effects=True, vmem_limit_bytes=40 * 2**20
        ),
        cost_estimate=pl.CostEstimate(flops=heads * 60 * 2 * 128**3, bytes_accessed=2**22, transcendentals=0),
    )(*major, gates)
    return jnp.transpose(mixed, (1, 0, 2))


def solution(mesh):
    placed = P(("outer", "inner"), None, None)
    return jax.shard_map(
        functools.partial(shards, mesh.shape["outer"], mesh.shape["inner"]),
        mesh=mesh,
        in_specs=(placed, placed, placed, P(("outer", "inner"), None)),
        out_specs=placed,
        check_vma=False,
    )
```

```python
import functools

import jax
import jax.numpy as jnp
from jax import lax
from jax.experimental import pallas as pl
from jax.experimental.pallas import tpu as pltpu
from jax.sharding import PartitionSpec as P

SPAN = 128
GROUP = 4
F32 = jnp.float32
BF16 = jnp.bfloat16


def halves(x):
    high = x.astype(BF16)
    return high, (x - high.astype(F32)).astype(BF16)


def dot(a, b):
    return jnp.dot(a, b, preferred_element_type=F32)


def dot_halves(a, b):
    (ah, al), (bh, bl) = a, b
    return dot(jnp.concatenate([ah, al], 1), jnp.concatenate([bh, bh], 0)) + dot(ah, bl)


def dot_exact(a, b):
    ah, al = a
    return dot(jnp.concatenate([ah, al], 1), jnp.concatenate([b, b], 0))


def block_map(keys, value, brow, rows, cols):
    eye = rows == cols
    width = keys[0].shape[1]
    count = range(len(keys))
    gram = [lax.dot_general(x, x, (((1,), (1,)), ((), ())), preferred_element_type=F32) for x in keys]
    kf = [x.astype(F32) for x in keys]
    krow = [lax.rsqrt(jnp.sum(jnp.where(eye, x, 0.0), axis=0, keepdims=True) + 1e-6) for x in gram]
    kcol = [lax.rsqrt(jnp.sum(x * x, axis=1, keepdims=True) + 1e-6) for x in kf]
    bcol = [jnp.sum(jnp.where(eye, x, 0.0), axis=1, keepdims=True) for x in brow]
    lower = [jnp.where(rows > cols, gram[i] * (bcol[i] * kcol[i]) * krow[i], 0.0) for i in count]
    split = [halves(x) for x in lower]

    def merge_mask(level):
        return ((rows >> (level + 1)) == (cols >> (level + 1))) & (((rows >> level) & 1) == 1) & (((cols >> level) & 1) == 0)

    first = merge_mask(0)
    inverse = [jnp.where(eye, 1.0, 0.0) - jnp.where(first, x, 0.0) for x in lower]
    zero = jnp.zeros((), BF16)
    for level in range(1, (SPAN - 1).bit_length()):
        mask = merge_mask(level)
        part = [(jnp.where(mask, h, zero), jnp.where(mask, l, zero)) for h, l in split]
        inv = [halves(x) for x in inverse]
        inner = [dot_halves(part[i], inv[i]) for i in count]
        inner = [halves(x) for x in inner]
        change = [dot_halves(inv[i], inner[i]) for i in count]
        inverse = [inverse[i] - change[i] for i in count]
    for_keys = [halves(inverse[i] * (brow[i] * krow[i])) for i in count]
    for_value = [halves(inverse[i] * brow[i]) for i in count]
    weights = [dot_exact(for_keys[i], keys[i]) for i in count]
    updates = [dot_exact(for_value[i], value[i]) for i in count]
    solved = [jnp.concatenate([weights[i], updates[i]], 1) for i in count]
    scaled = [halves(solved[i] * kcol[i]) for i in count]
    written = [
        lax.dot_general(
            jnp.concatenate([keys[i], keys[i]], 0),
            jnp.concatenate(scaled[i], 0),
            (((0,), (0,)), ((), ())),
            preferred_element_type=F32,
        )
        for i in count
    ]
    trans = [jnp.where(eye, 1.0, 0.0) - x[:, :width] for x in written]
    return trans, [x[:, width:] for x in written], solved, krow


def block_reads(query, keys, solved, krow, rows, cols):
    width = keys[0].shape[1]
    count = range(len(keys))
    raw = [
        lax.dot_general(q, k, (((1,), (1,)), ((), ())), preferred_element_type=F32) for q, k in zip(query, keys)
    ]
    qf = [x.astype(F32) for x in query]
    qcol = [lax.rsqrt(jnp.sum(x * x, axis=1, keepdims=True) + 1e-6) for x in qf]
    scores = [halves(jnp.where(rows >= cols, raw[i] * qcol[i] * krow[i], 0.0)) for i in count]
    solved = [halves(x) for x in solved]
    seen = [dot_halves(scores[i], solved[i]) for i in count]
    return [qf[i] * qcol[i] - seen[i][:, :width] for i in count], [x[:, width:] for x in seen]


def kernel(outer, inner, q_ref, k_ref, v_ref, b_ref, o_ref, pair, outgoing, solved, norms, whole, jump, first, came, goes, middle, side, ab_send, ab_recv, chain_send, chain_recv, side_send, side_recv):
    heads = q_ref.shape[0]
    owned = heads // 2
    each = GROUP // 2
    groups = owned // each
    total = outer * inner
    me = lax.axis_index("outer") * inner + lax.axis_index("inner")
    core, chip, chips = lax.rem(me, 2), me // 2, total // 2
    after, before, sibling = lax.rem(me + 2, total), lax.rem(me + total - 2, total), me + 1 - 2 * core

    def place(index):
        return (index // inner, lax.rem(index, inner))

    barrier = pltpu.get_barrier_semaphore()
    for other in (after, before, sibling):
        pl.semaphore_signal(barrier, inc=1, device_id=place(other), device_id_type=pl.DeviceIdType.MESH)
    pl.semaphore_wait(barrier, 3)

    def send(src, dst, send_sem, recv_sem, to):
        return pltpu.make_async_remote_copy(
            src_ref=src,
            dst_ref=dst,
            send_sem=send_sem,
            recv_sem=recv_sem,
            device_id=place(to),
            device_id_type=pl.DeviceIdType.MESH,
        )

    def give(m):
        return send(outgoing.at[m], pair.at[m, core], ab_send.at[m], ab_recv.at[m], sibling)

    def take(m):
        return send(outgoing.at[m], pair.at[m, 1 - core], ab_send.at[m], ab_recv.at[m], sibling)

    def hop(m):
        return send(goes.at[m], came.at[m], chain_send.at[m], chain_recv.at[m], after)

    def aside(src, m):
        return send(src.at[m], side.at[m], side_send.at[m], side_recv.at[m], sibling)

    @pl.when(chip == 0)
    def _():
        came[...] = jnp.zeros_like(came)

    def masks():
        return [lax.broadcasted_iota(jnp.int32, (SPAN, SPAN), axis) for axis in (0, 1)]

    def group(g):
        ms = [g * each + j for j in range(each)]
        return ms, [core * owned + m for m in ms], [(1 - core) * owned + m for m in ms]

    def prepare(g):
        ms, mine, theirs = group(g)
        hs = mine + theirs
        a, b, wu, krow = block_map(*([ref[h] for h in hs] for ref in (k_ref, v_ref, b_ref)), *masks())
        for j, h in enumerate(hs):
            solved[h] = wu[j]
            norms[h] = krow[j]
        for j, m in enumerate(ms):
            outgoing[m, :SPAN] = a[each + j]
            outgoing[m, SPAN:] = b[each + j]
        for m in ms:
            give(m).start()
        for j, m in enumerate(ms):
            pair[m, core, :SPAN] = a[j]
            pair[m, core, SPAN:] = b[j]

    def compose(g):
        ms, _, _ = group(g)
        for m in ms:
            take(m).wait_recv()
        early = [halves(jnp.concatenate([pair[m, 0, :SPAN], pair[m, 0, SPAN:]], 1)) for m in ms]
        late = [halves(pair[m, 1, :SPAN]) for m in ms]
        both = [dot_halves(x, y) for x, y in zip(late, early)]
        for j, m in enumerate(ms):
            whole[m] = jnp.concatenate(halves(both[j][:, :SPAN]), 1)
            jump[m] = both[j][:, SPAN:] + pair[m, 1, SPAN:]
            first[m] = jnp.concatenate([x[:, :SPAN] for x in early[j]], 1)

    def apply(linear, state, constant):
        high, low = state
        return constant + dot(linear, jnp.concatenate([high, high], 0)) + dot(linear[:, :SPAN], low)

    def pass_on(g):
        ms, _, _ = group(g)
        for m in ms:
            @pl.when(chip > 0)
            def _():
                hop(m).wait_recv()

            goes[m] = apply(whole[m], halves(came[m]), jump[m])

            @pl.when(chip < chips - 1)
            def _():
                hop(m).start()

            @pl.when(core == 1)
            def _():
                aside(came, m).start()

        for m in ms:
            middle[m] = apply(first[m], halves(came[m]), pair[m, 0, SPAN:])

        @pl.when(core == 0)
        def _():
            for m in ms:
                aside(middle, m).start()

    def read_terms(g):
        _, mine, theirs = group(g)
        hs = mine + theirs
        p, o = block_reads([q_ref[h] for h in hs], [k_ref[h] for h in hs], [solved[h] for h in hs], [norms[h] for h in hs], *masks())
        for j, h in enumerate(hs):
            solved[h] = jnp.concatenate([p[j], o[j]], 1)

    def put(hs, states):
        terms = [solved[h] for h in hs]
        states = [halves(x) for x in states]
        mixed = [x[:, SPAN:] + dot_halves(halves(x[:, :SPAN]), y) for x, y in zip(terms, states)]
        for h, x in zip(hs, mixed):
            o_ref[h] = x.astype(BF16)

    def finish(g):
        ms, mine, theirs = group(g)
        put(mine, [jnp.where(core == 0, came[m], middle[m]) for m in ms])
        for m in ms:
            aside(middle, m).wait_recv()
        put(theirs, [side[m] for m in ms])

    ahead = jnp.minimum(groups, 1 + chip // 2)
    late = jnp.where(chip < chips // 2, groups + ahead, 0)
    last = jnp.maximum(late, ahead + 1)

    def step(i, carry):
        @pl.when(i < groups)
        def _():
            prepare(i)

        @pl.when((i >= late) & (i < late + groups))
        def _():
            read_terms(i - late)

        @pl.when((i >= 1) & (i <= groups))
        def _():
            compose(i - 1)

        @pl.when((i >= ahead) & (i < ahead + groups))
        def _():
            pass_on(i - ahead)

        @pl.when((i >= last) & (i < last + groups))
        def _():
            finish(i - last)

        return carry

    lax.fori_loop(0, groups + last, step, 0)

    def drain(m, carry):
        give(m).wait_send()
        aside(middle, m).wait_send()

        @pl.when(chip < chips - 1)
        def _():
            hop(m).wait_send()

        return carry

    lax.fori_loop(0, owned, drain, 0)


def shards(outer, inner, query, keys, value, beta):
    tokens, heads, width = query.shape
    major = [jnp.transpose(x, (1, 0, 2)) for x in (query, keys, value)]
    gates = jnp.transpose(beta.astype(F32), (1, 0)).reshape(heads, 1, tokens)
    half = heads // 2
    vmem = pl.BlockSpec(memory_space=pltpu.VMEM)
    mixed = pl.pallas_call(
        functools.partial(kernel, outer, inner),
        out_shape=jax.ShapeDtypeStruct((heads, tokens, width), BF16),
        in_specs=[vmem] * 4,
        out_specs=vmem,
        scratch_shapes=[
            pltpu.VMEM((half, 2, 2 * width, width), F32),
            pltpu.VMEM((half, 2 * width, width), F32),
            pltpu.VMEM((heads, tokens, 2 * width), F32),
            pltpu.VMEM((heads, 1, tokens), F32),
            pltpu.VMEM((half, width, 2 * width), BF16),
            pltpu.VMEM((half, width, width), F32),
            pltpu.VMEM((half, width, 2 * width), BF16),
            *[pltpu.VMEM((half, width, width), F32)] * 4,
            *[pltpu.SemaphoreType.DMA((half,))] * 6,
        ],
        compiler_params=pltpu.CompilerParams(
            collective_id=0, has_side_effects=True, vmem_limit_bytes=40 * 2**20
        ),
        cost_estimate=pl.CostEstimate(flops=heads * 60 * 2 * 128**3, bytes_accessed=2**22, transcendentals=0),
    )(*major, gates)
    return jnp.transpose(mixed, (1, 0, 2))


def solution(mesh):
    placed = P(("outer", "inner"), None, None)
    return jax.shard_map(
        functools.partial(shards, mesh.shape["outer"], mesh.shape["inner"]),
        mesh=mesh,
        in_specs=(placed, placed, placed, P(("outer", "inner"), None)),
        out_specs=placed,
        check_vma=False,
    )
```

```python
import functools

import jax
import jax.numpy as jnp
from jax import lax
from jax.experimental import pallas as pl
from jax.experimental.pallas import tpu as pltpu
from jax.sharding import PartitionSpec as P

SPAN = 128
F32 = jnp.float32
BF16 = jnp.bfloat16


def halves(x):
    high = x.astype(BF16)
    return high, (x - high.astype(F32)).astype(BF16)


def dot(a, b):
    return jnp.dot(a, b, preferred_element_type=F32)


def dot_halves(a, b):
    (ah, al), (bh, bl) = a, b
    return dot(jnp.concatenate([ah, al], 1), jnp.concatenate([bh, bh], 0)) + dot(ah, bl)


def dot_exact(a, b):
    ah, al = a
    return dot(jnp.concatenate([ah, al], 1), jnp.concatenate([b, b], 0))


def block_map(keys, value, brow, rows, cols):
    eye = rows == cols
    width = keys[0].shape[1]
    count = range(len(keys))
    gram = [lax.dot_general(x, x, (((1,), (1,)), ((), ())), preferred_element_type=F32) for x in keys]
    kf = [x.astype(F32) for x in keys]
    krow = [lax.rsqrt(jnp.sum(jnp.where(eye, x, 0.0), axis=0, keepdims=True) + 1e-6) for x in gram]
    kcol = [lax.rsqrt(jnp.sum(x * x, axis=1, keepdims=True) + 1e-6) for x in kf]
    bcol = [jnp.sum(jnp.where(eye, x, 0.0), axis=1, keepdims=True) for x in brow]
    lower = [jnp.where(rows > cols, gram[i] * (bcol[i] * kcol[i]) * krow[i], 0.0) for i in count]
    split = [halves(x) for x in lower]

    def merge_mask(level):
        return ((rows >> (level + 1)) == (cols >> (level + 1))) & (((rows >> level) & 1) == 1) & (((cols >> level) & 1) == 0)

    first = merge_mask(0)
    inverse = [jnp.where(eye, 1.0, 0.0) - jnp.where(first, x, 0.0) for x in lower]
    zero = jnp.zeros((), BF16)
    for level in range(1, (SPAN - 1).bit_length()):
        mask = merge_mask(level)
        part = [(jnp.where(mask, h, zero), jnp.where(mask, l, zero)) for h, l in split]
        inv = [halves(x) for x in inverse]
        inner = [dot_halves(part[i], inv[i]) for i in count]
        inner = [halves(x) for x in inner]
        change = [dot_halves(inv[i], inner[i]) for i in count]
        inverse = [inverse[i] - change[i] for i in count]
    for_keys = [halves(inverse[i] * (brow[i] * krow[i])) for i in count]
    for_value = [halves(inverse[i] * brow[i]) for i in count]
    weights = [dot_exact(for_keys[i], keys[i]) for i in count]
    updates = [dot_exact(for_value[i], value[i]) for i in count]
    solved = [jnp.concatenate([weights[i], updates[i]], 1) for i in count]
    scaled = [halves(solved[i] * kcol[i]) for i in count]
    written = [
        lax.dot_general(
            jnp.concatenate([keys[i], keys[i]], 0),
            jnp.concatenate(scaled[i], 0),
            (((0,), (0,)), ((), ())),
            preferred_element_type=F32,
        )
        for i in count
    ]
    trans = [jnp.where(eye, 1.0, 0.0) - x[:, :width] for x in written]
    return trans, [x[:, width:] for x in written], solved, krow


def block_reads(query, keys, solved, krow, rows, cols):
    width = keys[0].shape[1]
    count = range(len(keys))
    raw = [
        lax.dot_general(q, k, (((1,), (1,)), ((), ())), preferred_element_type=F32) for q, k in zip(query, keys)
    ]
    qf = [x.astype(F32) for x in query]
    qcol = [lax.rsqrt(jnp.sum(x * x, axis=1, keepdims=True) + 1e-6) for x in qf]
    scores = [halves(jnp.where(rows >= cols, raw[i] * qcol[i] * krow[i], 0.0)) for i in count]
    solved = [halves(x) for x in solved]
    seen = [dot_halves(scores[i], solved[i]) for i in count]
    return [qf[i] * qcol[i] - seen[i][:, :width] for i in count], [x[:, width:] for x in seen]


def kernel(
    outer, inner, q_ref, k_ref, v_ref, b_ref, o_ref,
    pair, outgoing, solved, norms, first, chip_map, cross, whole, jump, inside, came, goes, start, chip_start, middle, side,
    ab_send, ab_recv, side_send, side_recv, cross_send, cross_recv, down_send, down_recv, chain_send, chain_recv,
):
    heads = q_ref.shape[0]
    owned = heads // 2
    chips = inner // 2
    groups = owned // chips
    total = outer * inner
    stage, place_in = lax.axis_index("outer"), lax.axis_index("inner")
    core, chip = lax.rem(place_in, 2), place_in // 2
    after, before = lax.rem(stage + 1, outer), lax.rem(stage + outer - 1, outer)
    sibling = (stage, place_in + 1 - 2 * core)

    def turned(d):
        return lax.rem(chip + d, chips)

    def beside(other):
        return (stage, other * 2 + core)

    barrier = pltpu.get_barrier_semaphore()
    met = [(after, place_in), (before, place_in), sibling] + [beside(turned(d)) for d in range(1, chips)]
    for other in met:
        pl.semaphore_signal(barrier, inc=1, device_id=other, device_id_type=pl.DeviceIdType.MESH)
    pl.semaphore_wait(barrier, len(met))

    def send(src, dst, send_sem, recv_sem, to):
        return pltpu.make_async_remote_copy(
            src_ref=src,
            dst_ref=dst,
            send_sem=send_sem,
            recv_sem=recv_sem,
            device_id=to,
            device_id_type=pl.DeviceIdType.MESH,
        )

    def give(m):
        return send(outgoing.at[m], pair.at[m, core], ab_send.at[m], ab_recv.at[m], sibling)

    def across(g, d):
        other, at = turned(d), g * (chips - 1) + d - 1
        return send(chip_map.at[other * groups + g], cross.at[g, chip], cross_send.at[at], cross_recv.at[at], beside(other))

    def across_in(g, d):
        other, at = turned(chips - d), g * (chips - 1) + d - 1
        return send(chip_map.at[g], cross.at[g, other], cross_send.at[at], cross_recv.at[at], beside(other))

    def hop(g):
        return send(goes.at[g], came.at[g], chain_send.at[g], chain_recv.at[g], (after, place_in))

    def down(g, d):
        other, at = turned(d), g * (chips - 1) + d - 1
        return send(start.at[g, other], chip_start.at[chip * groups + g], down_send.at[at], down_recv.at[at], beside(other))

    def down_in(g, d):
        other, at = turned(chips - d), g * (chips - 1) + d - 1
        return send(start.at[g, other], chip_start.at[other * groups + g], down_send.at[at], down_recv.at[at], beside(other))

    def aside(src, m):
        return send(src.at[m], side.at[m], side_send.at[m], side_recv.at[m], sibling)

    @pl.when(stage == 0)
    def _():
        came[...] = jnp.zeros_like(came)

    def masks():
        return [lax.broadcasted_iota(jnp.int32, (SPAN, SPAN), axis) for axis in (0, 1)]

    def group(g):
        ms = [c * groups + g for c in range(chips)]
        return ms, [core * owned + m for m in ms], [(1 - core) * owned + m for m in ms]

    def prepare(g):
        ms, mine, theirs = group(g)
        hs = mine + theirs
        a, b, wu, krow = block_map(*([ref[h] for h in hs] for ref in (k_ref, v_ref, b_ref)), *masks())
        for j, h in enumerate(hs):
            solved[h] = wu[j]
            norms[h] = krow[j]
        for j, m in enumerate(ms):
            outgoing[m, :SPAN] = a[chips + j]
            outgoing[m, SPAN:] = b[chips + j]
        for m in ms:
            give(m).start()
        for j, m in enumerate(ms):
            pair[m, core, :SPAN] = a[j]
            pair[m, core, SPAN:] = b[j]

    def compose(g):
        ms, _, _ = group(g)
        for m in ms:
            send(outgoing.at[m], pair.at[m, 1 - core], ab_send.at[m], ab_recv.at[m], sibling).wait_recv()
        early = [halves(jnp.concatenate([pair[m, 0, :SPAN], pair[m, 0, SPAN:]], 1)) for m in ms]
        late = [halves(pair[m, 1, :SPAN]) for m in ms]
        both = [dot_halves(x, y) for x, y in zip(late, early)]
        for j, m in enumerate(ms):
            chip_map[m, :SPAN] = both[j][:, :SPAN]
            chip_map[m, SPAN:] = both[j][:, SPAN:] + pair[m, 1, SPAN:]
        for d in range(1, chips):
            across(g, d).start()
        for j, m in enumerate(ms):
            first[m] = jnp.concatenate([x[:, :SPAN] for x in early[j]], 1)
        cross[g, chip] = chip_map[chip * groups + g]

    def compose_chips(g):
        for d in range(1, chips):
            across_in(g, d).wait_recv()
        both = jnp.concatenate([cross[g, 0, :SPAN], cross[g, 0, SPAN:]], 1)
        for c in range(1, chips):
            split = halves(both)
            if c == 1:
                inside[g, 0] = jnp.concatenate([x[:, :SPAN] for x in split], 1)
            late = halves(cross[g, c, :SPAN])
            if c < chips - 1:
                inside[g, c] = jnp.concatenate(late, 1)
            moved = dot_halves(late, split)
            both = jnp.concatenate([moved[:, :SPAN], moved[:, SPAN:] + cross[g, c, SPAN:]], 1)
        whole[g] = jnp.concatenate(halves(both[:, :SPAN]), 1)
        jump[g] = both[:, SPAN:]

    def apply(linear, state, constant):
        high, low = halves(state)
        return constant + dot(linear, jnp.concatenate([high, high], 0)) + dot(linear[:, :SPAN], low)

    def pass_on(g):
        @pl.when(stage > 0)
        def _():
            hop(g).wait_recv()

        state = came[g]
        goes[g] = apply(whole[g], state, jump[g])

        @pl.when(stage < outer - 1)
        def _():
            hop(g).start()

        for c in range(chips):
            start[g, c] = state
            if c < chips - 1:
                state = apply(inside[g, c], state, cross[g, c, SPAN:])
        for d in range(1, chips):
            down(g, d).start()
        chip_start[chip * groups + g] = start[g, chip]

    def spread(g):
        ms, _, _ = group(g)
        for d in range(1, chips):
            down_in(g, d).wait_recv()

        @pl.when(core == 1)
        def _():
            for m in ms:
                aside(chip_start, m).start()

        for m in ms:
            middle[m] = apply(first[m], chip_start[m], pair[m, 0, SPAN:])

        @pl.when(core == 0)
        def _():
            for m in ms:
                aside(middle, m).start()

    def read_terms(g):
        _, mine, theirs = group(g)
        hs = mine + theirs
        p, o = block_reads(*([ref[h] for h in hs] for ref in (q_ref, k_ref, solved, norms)), *masks())
        for j, h in enumerate(hs):
            solved[h] = jnp.concatenate([p[j], o[j]], 1)

    def put(hs, states):
        terms = [solved[h] for h in hs]
        states = [halves(x) for x in states]
        mixed = [x[:, SPAN:] + dot_halves(halves(x[:, :SPAN]), y) for x, y in zip(terms, states)]
        for h, x in zip(hs, mixed):
            o_ref[h] = x.astype(BF16)

    def finish(g):
        ms, mine, theirs = group(g)
        put(mine, [jnp.where(core == 0, chip_start[m], middle[m]) for m in ms])
        for m in ms:
            aside(middle, m).wait_recv()
        put(theirs, [side[m] for m in ms])

    ahead = jnp.minimum(groups, 2 + 3 * stage // 4)
    late = jnp.where(stage < outer // 4, groups + ahead, 0)
    last = jnp.maximum(late, ahead + 2)

    def step(i, carry):
        def at(delay, do):
            @pl.when((i >= delay) & (i < delay + groups))
            def _():
                do(i - delay)

        at(0, prepare)
        at(late, read_terms)
        at(1, compose)
        at(2, compose_chips)
        at(ahead, pass_on)
        at(ahead + 1, spread)
        at(last, finish)
        return carry

    lax.fori_loop(0, groups + last, step, 0)

    def drain(m, carry):
        give(m).wait_send()
        aside(middle, m).wait_send()
        return carry

    lax.fori_loop(0, owned, drain, 0)

    def drain_chain(g, carry):
        for d in range(1, chips):
            across(g, d).wait_send()
            down(g, d).wait_send()

        @pl.when(stage < outer - 1)
        def _():
            hop(g).wait_send()

        return carry

    lax.fori_loop(0, groups, drain_chain, 0)


def shards(outer, inner, query, keys, value, beta):
    tokens, heads, width = query.shape
    major = [jnp.transpose(x, (1, 0, 2)) for x in (query, keys, value)]
    gates = jnp.transpose(beta.astype(F32), (1, 0)).reshape(heads, 1, tokens)
    half, chips = heads // 2, inner // 2
    groups = half // chips
    vmem = pl.BlockSpec(memory_space=pltpu.VMEM)
    mixed = pl.pallas_call(
        functools.partial(kernel, outer, inner),
        out_shape=jax.ShapeDtypeStruct((heads, tokens, width), BF16),
        in_specs=[vmem] * 4,
        out_specs=vmem,
        scratch_shapes=[
            pltpu.VMEM((half, 2, 2 * width, width), F32),
            pltpu.VMEM((half, 2 * width, width), F32),
            pltpu.VMEM((heads, tokens, 2 * width), F32),
            pltpu.VMEM((heads, 1, tokens), F32),
            pltpu.VMEM((half, width, 2 * width), BF16),
            pltpu.VMEM((half, 2 * width, width), F32),
            pltpu.VMEM((groups, chips, 2 * width, width), F32),
            pltpu.VMEM((groups, width, 2 * width), BF16),
            pltpu.VMEM((groups, width, width), F32),
            pltpu.VMEM((groups, chips - 1, width, 2 * width), BF16),
            pltpu.VMEM((groups, width, width), F32),
            pltpu.VMEM((groups, width, width), F32),
            pltpu.VMEM((groups, chips, width, width), F32),
            *[pltpu.VMEM((half, width, width), F32)] * 3,
            *[pltpu.SemaphoreType.DMA((half,))] * 4,
            *[pltpu.SemaphoreType.DMA((groups * (chips - 1),))] * 4,
            *[pltpu.SemaphoreType.DMA((groups,))] * 2,
        ],
        compiler_params=pltpu.CompilerParams(
            collective_id=0, has_side_effects=True, vmem_limit_bytes=40 * 2**20
        ),
        cost_estimate=pl.CostEstimate(flops=heads * 60 * 2 * 128**3, bytes_accessed=2**22, transcendentals=0),
    )(*major, gates)
    return jnp.transpose(mixed, (1, 0, 2))


def solution(mesh):
    placed = P(("outer", "inner"), None, None)
    return jax.shard_map(
        functools.partial(shards, mesh.shape["outer"], mesh.shape["inner"]),
        mesh=mesh,
        in_specs=(placed, placed, placed, P(("outer", "inner"), None)),
        out_specs=placed,
        check_vma=False,
    )
```

```python
import functools

import jax
import jax.numpy as jnp
from jax import lax
from jax.experimental import pallas as pl
from jax.experimental.pallas import tpu as pltpu
from jax.sharding import PartitionSpec as P

SPAN = 128
BASE = 16
F32 = jnp.float32
BF16 = jnp.bfloat16


def halves(x):
    high = x.astype(BF16)
    return high, (x - high.astype(F32)).astype(BF16)


def dot(a, b):
    return jnp.dot(a, b, preferred_element_type=F32)


def dot_halves(a, b):
    (ah, al), (bh, bl) = a, b
    return dot(jnp.concatenate([ah, al], 1), jnp.concatenate([bh, bh], 0)) + dot(ah, bl)


def dot_exact(a, b):
    ah, al = a
    return dot(jnp.concatenate([ah, al], 1), jnp.concatenate([b, b], 0))


def odd_rows(x, size):
    return jnp.concatenate([x[at : at + size] for at in range(size, SPAN, 2 * size)], 0)


def below(x, size):
    shape = (SPAN // 2, SPAN)
    block = lax.broadcasted_iota(jnp.int32, shape, 0) // size
    return jnp.where(lax.broadcasted_iota(jnp.int32, shape, 1) // size == 2 * block, odd_rows(x, size), jnp.zeros((), x.dtype))


def spaced(x, size):
    zeros = jnp.zeros((size, x.shape[1]), x.dtype)
    return jnp.concatenate([y for at in range(0, SPAN // 2, size) for y in (zeros, x[at : at + size])], 0)


def minus_odd_rows(x, change, size):
    out = []
    for at in range(0, SPAN // 2, size):
        out += [x[2 * at : 2 * at + size], x[2 * at + size : 2 * at + 2 * size] - change[at : at + size]]
    return jnp.concatenate(out, 0)


def diagonal_inverses(lower, pick):
    count = len(lower)
    row, lane = (lax.broadcasted_iota(jnp.int32, (BASE, SPAN), axis) for axis in (0, 1))
    here = [lane // BASE == k for k in range(SPAN // BASE)]
    beside = [sum(jnp.where(here[k], x[k * BASE : (k + 1) * BASE], 0.0) for k in range(SPAN // BASE)) for x in lower]
    split = [halves(x) for x in beside]
    spread = dot(jnp.concatenate([x for x, _ in split] + [x for _, x in split], 0), pick[...])
    spread = spread[: count * BASE] + spread[count * BASE :]
    found = [jnp.where(lane % BASE == row, 1.0, 0.0)] * count
    for c in range(BASE - 1):
        for i in range(count):
            factor = spread[i * BASE : (i + 1) * BASE, c * SPAN : (c + 1) * SPAN]
            found[i] = found[i] - factor * found[i][c : c + 1]
    return [jnp.concatenate([jnp.where(x, y, 0.0) for x in here], 0) for y in found]


def block_map(keys, value, brow, rows, cols, pick):
    eye = rows == cols
    width = keys[0].shape[1]
    count = range(len(keys))
    gram = [lax.dot_general(x, x, (((1,), (1,)), ((), ())), preferred_element_type=F32) for x in keys]
    kf = [x.astype(F32) for x in keys]
    krow = [lax.rsqrt(jnp.sum(jnp.where(eye, x, 0.0), axis=0, keepdims=True) + 1e-6) for x in gram]
    kcol = [lax.rsqrt(jnp.sum(x * x, axis=1, keepdims=True) + 1e-6) for x in kf]
    bcol = [jnp.sum(jnp.where(eye, x, 0.0), axis=1, keepdims=True) for x in brow]
    lower = [jnp.where(rows > cols, gram[i] * (bcol[i] * kcol[i]) * krow[i], 0.0) for i in count]
    inverse = diagonal_inverses(lower, pick)
    split = [halves(x) for x in lower]
    size = BASE
    while size < SPAN:
        inv = [halves(x) for x in inverse]
        part = [tuple(below(x, size) for x in y) for y in split]
        inner = [halves(dot_halves(part[i], inv[i])) for i in count]
        inner = [tuple(spaced(x, size) for x in y) for y in inner]
        change = [dot_halves(tuple(odd_rows(x, size) for x in inv[i]), inner[i]) for i in count]
        inverse = [minus_odd_rows(inverse[i], change[i], size) for i in count]
        size *= 2
    for_keys = [halves(inverse[i] * (brow[i] * krow[i])) for i in count]
    for_value = [halves(inverse[i] * brow[i]) for i in count]
    weights = [dot_exact(for_keys[i], keys[i]) for i in count]
    updates = [dot_exact(for_value[i], value[i]) for i in count]
    solved = [jnp.concatenate([weights[i], updates[i]], 1) for i in count]
    scaled = [halves(solved[i] * kcol[i]) for i in count]
    turned = [jnp.transpose(x) for x in keys]
    written = [dot(jnp.concatenate([turned[i]] * 2, 1), jnp.concatenate(scaled[i], 0)) for i in count]
    trans = [jnp.where(eye, 1.0, 0.0) - x[:, :width] for x in written]
    return trans, [x[:, width:] for x in written], solved, krow


def block_reads(query, keys, solved, krow, rows, cols):
    width = keys[0].shape[1]
    count = range(len(keys))
    raw = [
        lax.dot_general(q, k, (((1,), (1,)), ((), ())), preferred_element_type=F32) for q, k in zip(query, keys)
    ]
    qf = [x.astype(F32) for x in query]
    qcol = [lax.rsqrt(jnp.sum(x * x, axis=1, keepdims=True) + 1e-6) for x in qf]
    scores = [halves(jnp.where(rows >= cols, raw[i] * qcol[i] * krow[i], 0.0)) for i in count]
    solved = [halves(x) for x in solved]
    seen = [dot_halves(scores[i], solved[i]) for i in count]
    return [qf[i] * qcol[i] - seen[i][:, :width] for i in count], [x[:, width:] for x in seen]


def kernel(
    outer, inner, q_ref, k_ref, v_ref, b_ref, o_ref,
    pair, outgoing, solved, norms, first, chip_map, cross, whole, jump, inside, came, goes, start, chip_start, middle, side, pick,
    ab_send, ab_recv, side_send, side_recv, cross_send, cross_recv, down_send, down_recv, chain_send, chain_recv,
):
    heads = q_ref.shape[0]
    owned = heads // 2
    chips = inner // 2
    groups = owned // chips
    total = outer * inner
    stage, place_in = lax.axis_index("outer"), lax.axis_index("inner")
    core, chip = lax.rem(place_in, 2), place_in // 2
    after, before = lax.rem(stage + 1, outer), lax.rem(stage + outer - 1, outer)
    sibling = (stage, place_in + 1 - 2 * core)

    def turned(d):
        return lax.rem(chip + d, chips)

    def beside(other):
        return (stage, other * 2 + core)

    barrier = pltpu.get_barrier_semaphore()
    met = [(after, place_in), (before, place_in), sibling] + [beside(turned(d)) for d in range(1, chips)]
    for other in met:
        pl.semaphore_signal(barrier, inc=1, device_id=other, device_id_type=pl.DeviceIdType.MESH)
    pl.semaphore_wait(barrier, len(met))

    def send(src, dst, send_sem, recv_sem, to):
        return pltpu.make_async_remote_copy(
            src_ref=src,
            dst_ref=dst,
            send_sem=send_sem,
            recv_sem=recv_sem,
            device_id=to,
            device_id_type=pl.DeviceIdType.MESH,
        )

    def give(m):
        return send(outgoing.at[m], pair.at[m, core], ab_send.at[m], ab_recv.at[m], sibling)

    def across(g, d):
        other, at = turned(d), g * (chips - 1) + d - 1
        return send(chip_map.at[other * groups + g], cross.at[g, chip], cross_send.at[at], cross_recv.at[at], beside(other))

    def across_in(g, d):
        other, at = turned(chips - d), g * (chips - 1) + d - 1
        return send(chip_map.at[g], cross.at[g, other], cross_send.at[at], cross_recv.at[at], beside(other))

    def hop(g):
        return send(goes.at[g], came.at[g], chain_send.at[g], chain_recv.at[g], (after, place_in))

    def down(g, d):
        other, at = turned(d), g * (chips - 1) + d - 1
        return send(start.at[g, other], chip_start.at[chip * groups + g], down_send.at[at], down_recv.at[at], beside(other))

    def down_in(g, d):
        other, at = turned(chips - d), g * (chips - 1) + d - 1
        return send(start.at[g, other], chip_start.at[other * groups + g], down_send.at[at], down_recv.at[at], beside(other))

    def aside(src, m):
        return send(src.at[m], side.at[m], side_send.at[m], side_recv.at[m], sibling)

    @pl.when(stage == 0)
    def _():
        came[...] = jnp.zeros_like(came)

    def masks():
        return [lax.broadcasted_iota(jnp.int32, (SPAN, SPAN), axis) for axis in (0, 1)]

    row, lane = masks()
    for c in range(BASE - 1):
        pick[:, c * SPAN : (c + 1) * SPAN] = jnp.where(row == lane // BASE * BASE + c, 1.0, 0.0).astype(BF16)

    def group(g):
        ms = [c * groups + g for c in range(chips)]
        return ms, [core * owned + m for m in ms], [(1 - core) * owned + m for m in ms]

    def prepare(g):
        ms, mine, theirs = group(g)
        hs = mine + theirs
        a, b, wu, krow = block_map(*([ref[h] for h in hs] for ref in (k_ref, v_ref, b_ref)), *masks(), pick)
        for j, h in enumerate(hs):
            solved[h] = wu[j]
            norms[h] = krow[j]
        for j, m in enumerate(ms):
            outgoing[m, :SPAN] = a[chips + j]
            outgoing[m, SPAN:] = b[chips + j]
        for m in ms:
            give(m).start()
        for j, m in enumerate(ms):
            pair[m, core, :SPAN] = a[j]
            pair[m, core, SPAN:] = b[j]

    def compose(g):
        ms, _, _ = group(g)
        for m in ms:
            send(outgoing.at[m], pair.at[m, 1 - core], ab_send.at[m], ab_recv.at[m], sibling).wait_recv()
        early = [halves(jnp.concatenate([pair[m, 0, :SPAN], pair[m, 0, SPAN:]], 1)) for m in ms]
        late = [halves(pair[m, 1, :SPAN]) for m in ms]
        both = [dot_halves(x, y) for x, y in zip(late, early)]
        for j, m in enumerate(ms):
            chip_map[m, :SPAN] = both[j][:, :SPAN]
            chip_map[m, SPAN:] = both[j][:, SPAN:] + pair[m, 1, SPAN:]
        for d in range(1, chips):
            across(g, d).start()
        for j, m in enumerate(ms):
            first[m] = jnp.concatenate([x[:, :SPAN] for x in early[j]], 1)
        cross[g, chip] = chip_map[chip * groups + g]

    def compose_chips(g):
        for d in range(1, chips):
            across_in(g, d).wait_recv()
        both = jnp.concatenate([cross[g, 0, :SPAN], cross[g, 0, SPAN:]], 1)
        for c in range(1, chips):
            split = halves(both)
            if c == 1:
                inside[g, 0] = jnp.concatenate([x[:, :SPAN] for x in split], 1)
            late = halves(cross[g, c, :SPAN])
            if c < chips - 1:
                inside[g, c] = jnp.concatenate(late, 1)
            moved = dot_halves(late, split)
            both = jnp.concatenate([moved[:, :SPAN], moved[:, SPAN:] + cross[g, c, SPAN:]], 1)
        whole[g] = jnp.concatenate(halves(both[:, :SPAN]), 1)
        jump[g] = both[:, SPAN:]

    def apply(linear, state, constant):
        high, low = halves(state)
        return constant + dot(linear, jnp.concatenate([high, high], 0)) + dot(linear[:, :SPAN], low)

    def pass_on(g):
        @pl.when(stage > 0)
        def _():
            hop(g).wait_recv()

        state = came[g]
        goes[g] = apply(whole[g], state, jump[g])

        @pl.when(stage < outer - 1)
        def _():
            hop(g).start()

        for c in range(chips):
            start[g, c] = state
            if c < chips - 1:
                state = apply(inside[g, c], state, cross[g, c, SPAN:])
        for d in range(1, chips):
            down(g, d).start()
        chip_start[chip * groups + g] = start[g, chip]

    def spread(g):
        ms, _, _ = group(g)
        for d in range(1, chips):
            down_in(g, d).wait_recv()

        @pl.when(core == 1)
        def _():
            for m in ms:
                aside(chip_start, m).start()

        for m in ms:
            middle[m] = apply(first[m], chip_start[m], pair[m, 0, SPAN:])

        @pl.when(core == 0)
        def _():
            for m in ms:
                aside(middle, m).start()

    def read_terms(g):
        _, mine, theirs = group(g)
        hs = mine + theirs
        p, o = block_reads(*([ref[h] for h in hs] for ref in (q_ref, k_ref, solved, norms)), *masks())
        for j, h in enumerate(hs):
            solved[h] = jnp.concatenate([p[j], o[j]], 1)

    def put(hs, states):
        terms = [solved[h] for h in hs]
        states = [halves(x) for x in states]
        mixed = [x[:, SPAN:] + dot_halves(halves(x[:, :SPAN]), y) for x, y in zip(terms, states)]
        for h, x in zip(hs, mixed):
            o_ref[h] = x.astype(BF16)

    def finish(g):
        ms, mine, theirs = group(g)
        put(mine, [jnp.where(core == 0, chip_start[m], middle[m]) for m in ms])
        for m in ms:
            aside(middle, m).wait_recv()
        put(theirs, [side[m] for m in ms])

    ahead = jnp.minimum(groups, 2 + 3 * stage // 4)
    late = jnp.where(stage < outer // 4, groups + ahead, 0)
    last = jnp.maximum(late, ahead + 2)

    def step(i, carry):
        def at(delay, do):
            @pl.when((i >= delay) & (i < delay + groups))
            def _():
                do(i - delay)

        at(0, prepare)
        at(late, read_terms)
        at(1, compose)
        at(2, compose_chips)
        at(ahead, pass_on)
        at(ahead + 1, spread)
        at(last, finish)
        return carry

    lax.fori_loop(0, groups + last, step, 0)

    def drain(m, carry):
        give(m).wait_send()
        aside(middle, m).wait_send()
        return carry

    lax.fori_loop(0, owned, drain, 0)

    def drain_chain(g, carry):
        for d in range(1, chips):
            across(g, d).wait_send()
            down(g, d).wait_send()

        @pl.when(stage < outer - 1)
        def _():
            hop(g).wait_send()

        return carry

    lax.fori_loop(0, groups, drain_chain, 0)


def shards(outer, inner, query, keys, value, beta):
    tokens, heads, width = query.shape
    major = [jnp.transpose(x, (1, 0, 2)) for x in (query, keys, value)]
    gates = jnp.transpose(beta.astype(F32), (1, 0)).reshape(heads, 1, tokens)
    half, chips = heads // 2, inner // 2
    groups = half // chips
    vmem = pl.BlockSpec(memory_space=pltpu.VMEM)
    mixed = pl.pallas_call(
        functools.partial(kernel, outer, inner),
        out_shape=jax.ShapeDtypeStruct((heads, tokens, width), BF16),
        in_specs=[vmem] * 4,
        out_specs=vmem,
        scratch_shapes=[
            pltpu.VMEM((half, 2, 2 * width, width), F32),
            pltpu.VMEM((half, 2 * width, width), F32),
            pltpu.VMEM((heads, tokens, 2 * width), F32),
            pltpu.VMEM((heads, 1, tokens), F32),
            pltpu.VMEM((half, width, 2 * width), BF16),
            pltpu.VMEM((half, 2 * width, width), F32),
            pltpu.VMEM((groups, chips, 2 * width, width), F32),
            pltpu.VMEM((groups, width, 2 * width), BF16),
            pltpu.VMEM((groups, width, width), F32),
            pltpu.VMEM((groups, chips - 1, width, 2 * width), BF16),
            pltpu.VMEM((groups, width, width), F32),
            pltpu.VMEM((groups, width, width), F32),
            pltpu.VMEM((groups, chips, width, width), F32),
            *[pltpu.VMEM((half, width, width), F32)] * 3,
            pltpu.VMEM((SPAN, (BASE - 1) * SPAN), BF16),
            *[pltpu.SemaphoreType.DMA((half,))] * 4,
            *[pltpu.SemaphoreType.DMA((groups * (chips - 1),))] * 4,
            *[pltpu.SemaphoreType.DMA((groups,))] * 2,
        ],
        compiler_params=pltpu.CompilerParams(
            collective_id=0, has_side_effects=True, vmem_limit_bytes=40 * 2**20
        ),
        cost_estimate=pl.CostEstimate(flops=heads * 60 * 2 * 128**3, bytes_accessed=2**22, transcendentals=0),
    )(*major, gates)
    return jnp.transpose(mixed, (1, 0, 2))


def solution(mesh):
    placed = P(("outer", "inner"), None, None)
    return jax.shard_map(
        functools.partial(shards, mesh.shape["outer"], mesh.shape["inner"]),
        mesh=mesh,
        in_specs=(placed, placed, placed, P(("outer", "inner"), None)),
        out_specs=placed,
        check_vma=False,
    )
```

```python
import functools

import jax
import jax.numpy as jnp
from jax import lax
from jax.experimental import pallas as pl
from jax.experimental.pallas import tpu as pltpu
from jax.sharding import PartitionSpec as P

SPAN = 128
BASE = 16
F32 = jnp.float32
BF16 = jnp.bfloat16


def halves(x):
    high = x.astype(BF16)
    return high, (x - high.astype(F32)).astype(BF16)


def dot(a, b):
    return jnp.dot(a, b, preferred_element_type=F32)


def dot_halves(a, b):
    (ah, al), (bh, bl) = a, b
    return dot(jnp.concatenate([ah, al], 1), jnp.concatenate([bh, bh], 0)) + dot(ah, bl)


def dot_exact(a, b):
    ah, al = a
    return dot(jnp.concatenate([ah, al], 1), jnp.concatenate([b, b], 0))


def odd_rows(x, size):
    return jnp.concatenate([x[at : at + size] for at in range(size, SPAN, 2 * size)], 0)


def below(x, size):
    shape = (SPAN // 2, SPAN)
    block = lax.broadcasted_iota(jnp.int32, shape, 0) // size
    return jnp.where(lax.broadcasted_iota(jnp.int32, shape, 1) // size == 2 * block, odd_rows(x, size), jnp.zeros((), x.dtype))


def spaced(x, size):
    zeros = jnp.zeros((size, x.shape[1]), x.dtype)
    return jnp.concatenate([y for at in range(0, SPAN // 2, size) for y in (zeros, x[at : at + size])], 0)


def minus_odd_rows(x, change, size):
    out = []
    for at in range(0, SPAN // 2, size):
        out += [x[2 * at : 2 * at + size], x[2 * at + size : 2 * at + 2 * size] - change[at : at + size]]
    return jnp.concatenate(out, 0)


def diagonal_inverses(lower, pick):
    count = len(lower)
    row, lane = (lax.broadcasted_iota(jnp.int32, (BASE, SPAN), axis) for axis in (0, 1))
    here = [lane // BASE == k for k in range(SPAN // BASE)]
    beside = [sum(jnp.where(here[k], x[k * BASE : (k + 1) * BASE], 0.0) for k in range(SPAN // BASE)) for x in lower]
    split = [halves(x) for x in beside]
    spread = dot(jnp.concatenate([x for x, _ in split] + [x for _, x in split], 0), pick[...])
    spread = spread[: count * BASE] + spread[count * BASE :]
    found = [jnp.where(lane % BASE == row, 1.0, 0.0)] * count
    for c in range(BASE - 1):
        for i in range(count):
            factor = spread[i * BASE : (i + 1) * BASE, c * SPAN : (c + 1) * SPAN]
            found[i] = found[i] - factor * found[i][c : c + 1]
    return [jnp.concatenate([jnp.where(x, y, 0.0) for x in here], 0) for y in found]


def block_map(keys, value, brow, rows, cols, pick):
    eye = rows == cols
    width = keys[0].shape[1]
    count = range(len(keys))
    gram = [lax.dot_general(x, x, (((1,), (1,)), ((), ())), preferred_element_type=F32) for x in keys]
    kf = [x.astype(F32) for x in keys]
    krow = [lax.rsqrt(jnp.sum(jnp.where(eye, x, 0.0), axis=0, keepdims=True) + 1e-6) for x in gram]
    kcol = [lax.rsqrt(jnp.sum(x * x, axis=1, keepdims=True) + 1e-6) for x in kf]
    bcol = [jnp.sum(jnp.where(eye, x, 0.0), axis=1, keepdims=True) for x in brow]
    lower = [jnp.where(rows > cols, gram[i] * (bcol[i] * kcol[i]) * krow[i], 0.0) for i in count]
    inverse = diagonal_inverses(lower, pick)
    split = [halves(x) for x in lower]
    size = BASE
    while size < SPAN:
        inv = [halves(x) for x in inverse]
        part = [tuple(below(x, size) for x in y) for y in split]
        inner = [halves(dot_halves(part[i], inv[i])) for i in count]
        inner = [tuple(spaced(x, size) for x in y) for y in inner]
        change = [dot_halves(tuple(odd_rows(x, size) for x in inv[i]), inner[i]) for i in count]
        inverse = [minus_odd_rows(inverse[i], change[i], size) for i in count]
        size *= 2
    for_keys = [halves(inverse[i] * (brow[i] * krow[i])) for i in count]
    for_value = [halves(inverse[i] * brow[i]) for i in count]
    weights = [dot_exact(for_keys[i], keys[i]) for i in count]
    updates = [dot_exact(for_value[i], value[i]) for i in count]
    solved = [jnp.concatenate([weights[i], updates[i]], 1) for i in count]
    scaled = [halves(solved[i] * kcol[i]) for i in count]
    turned = [jnp.transpose(x) for x in keys]
    written = [dot(jnp.concatenate([turned[i]] * 2, 1), jnp.concatenate(scaled[i], 0)) for i in count]
    trans = [jnp.where(eye, 1.0, 0.0) - x[:, :width] for x in written]
    return trans, [x[:, width:] for x in written], solved, krow


def block_reads(query, keys, solved, krow, rows, cols):
    width = keys[0].shape[1]
    count = range(len(keys))
    raw = [
        lax.dot_general(q, k, (((1,), (1,)), ((), ())), preferred_element_type=F32) for q, k in zip(query, keys)
    ]
    qf = [x.astype(F32) for x in query]
    qcol = [lax.rsqrt(jnp.sum(x * x, axis=1, keepdims=True) + 1e-6) for x in qf]
    scores = [halves(jnp.where(rows >= cols, raw[i] * qcol[i] * krow[i], 0.0)) for i in count]
    solved = [halves(x) for x in solved]
    seen = [dot_halves(scores[i], solved[i]) for i in count]
    return [qf[i] * qcol[i] - seen[i][:, :width] for i in count], [x[:, width:] for x in seen]


def kernel(
    outer, inner, q_ref, k_ref, v_ref, b_ref, o_ref,
    pair, outgoing, solved, norms, first, chip_map, cross, whole, jump, inside, came, goes, start, chip_start, middle, side, pick,
    ab_send, ab_recv, side_send, side_recv, cross_send, cross_recv, down_send, down_recv, chain_send, chain_recv,
):
    heads = q_ref.shape[0]
    owned = heads // 2
    chips = inner // 2
    groups = owned // chips
    total = outer * inner
    stage, place_in = lax.axis_index("outer"), lax.axis_index("inner")
    core, chip = lax.rem(place_in, 2), place_in // 2
    after, before = lax.rem(stage + 1, outer), lax.rem(stage + outer - 1, outer)
    sibling = (stage, place_in + 1 - 2 * core)

    def turned(d):
        return lax.rem(chip + d, chips)

    def beside(other):
        return (stage, other * 2 + core)

    barrier = pltpu.get_barrier_semaphore()
    met = [(after, place_in), (before, place_in), sibling] + [beside(turned(d)) for d in range(1, chips)]
    for other in met:
        pl.semaphore_signal(barrier, inc=1, device_id=other, device_id_type=pl.DeviceIdType.MESH)
    pl.semaphore_wait(barrier, len(met))

    def send(src, dst, send_sem, recv_sem, to):
        return pltpu.make_async_remote_copy(
            src_ref=src,
            dst_ref=dst,
            send_sem=send_sem,
            recv_sem=recv_sem,
            device_id=to,
            device_id_type=pl.DeviceIdType.MESH,
        )

    def give(m):
        return send(outgoing.at[m], pair.at[m, core], ab_send.at[m], ab_recv.at[m], sibling)

    def across(g, d):
        other, at = turned(d), g * (chips - 1) + d - 1
        return send(chip_map.at[other * groups + g], cross.at[g, chip], cross_send.at[at], cross_recv.at[at], beside(other))

    def across_in(g, d):
        other, at = turned(chips - d), g * (chips - 1) + d - 1
        return send(chip_map.at[g], cross.at[g, other], cross_send.at[at], cross_recv.at[at], beside(other))

    def hop(g):
        return send(goes.at[g], came.at[g], chain_send.at[g], chain_recv.at[g], (after, place_in))

    def down(g, d):
        other, at = turned(d), g * (chips - 1) + d - 1
        return send(start.at[g, other], chip_start.at[chip * groups + g], down_send.at[at], down_recv.at[at], beside(other))

    def down_in(g, d):
        other, at = turned(chips - d), g * (chips - 1) + d - 1
        return send(start.at[g, other], chip_start.at[other * groups + g], down_send.at[at], down_recv.at[at], beside(other))

    def aside(src, m):
        return send(src.at[m], side.at[m], side_send.at[m], side_recv.at[m], sibling)

    @pl.when(stage == 0)
    def _():
        came[...] = jnp.zeros_like(came)

    def masks():
        return [lax.broadcasted_iota(jnp.int32, (SPAN, SPAN), axis) for axis in (0, 1)]

    row, lane = masks()
    for c in range(BASE - 1):
        pick[:, c * SPAN : (c + 1) * SPAN] = jnp.where(row == lane // BASE * BASE + c, 1.0, 0.0).astype(BF16)

    def group(g):
        ms = [c * groups + g for c in range(chips)]
        return ms, [core * owned + m for m in ms], [(1 - core) * owned + m for m in ms]

    def prepare(g):
        ms, mine, theirs = group(g)
        hs = mine + theirs
        a, b, wu, krow = block_map(*([ref[h] for h in hs] for ref in (k_ref, v_ref, b_ref)), *masks(), pick)
        for j, h in enumerate(hs):
            solved[h] = wu[j]
            norms[h] = krow[j]
        for j, m in enumerate(ms):
            outgoing[m, :SPAN] = a[chips + j]
            outgoing[m, SPAN:] = b[chips + j]
        for m in ms:
            give(m).start()
        for j, m in enumerate(ms):
            pair[m, core, :SPAN] = a[j]
            pair[m, core, SPAN:] = b[j]

    def compose(g):
        ms, _, _ = group(g)
        for m in ms:
            send(outgoing.at[m], pair.at[m, 1 - core], ab_send.at[m], ab_recv.at[m], sibling).wait_recv()
        early = [halves(jnp.concatenate([pair[m, 0, :SPAN], pair[m, 0, SPAN:]], 1)) for m in ms]
        late = [halves(pair[m, 1, :SPAN]) for m in ms]
        both = [dot_halves(x, y) for x, y in zip(late, early)]
        for j, m in enumerate(ms):
            chip_map[m, :SPAN] = both[j][:, :SPAN]
            chip_map[m, SPAN:] = both[j][:, SPAN:] + pair[m, 1, SPAN:]
        for d in range(1, chips):
            across(g, d).start()
        for j, m in enumerate(ms):
            first[m] = jnp.concatenate([x[:, :SPAN] for x in early[j]], 1)
        cross[g, chip] = chip_map[chip * groups + g]

    def compose_chips(g):
        for d in range(1, chips):
            across_in(g, d).wait_recv()
        both = jnp.concatenate([cross[g, 0, :SPAN], cross[g, 0, SPAN:]], 1)
        for c in range(1, chips):
            split = halves(both)
            if c == 1:
                inside[g, 0] = jnp.concatenate([x[:, :SPAN] for x in split], 1)
            late = halves(cross[g, c, :SPAN])
            if c < chips - 1:
                inside[g, c] = jnp.concatenate(late, 1)
            moved = dot_halves(late, split)
            both = jnp.concatenate([moved[:, :SPAN], moved[:, SPAN:] + cross[g, c, SPAN:]], 1)
        whole[g] = jnp.concatenate(halves(both[:, :SPAN]), 1)
        jump[g] = both[:, SPAN:]

    def apply(linear, state, constant):
        high, low = halves(state)
        return constant + dot(linear, jnp.concatenate([high, high], 0)) + dot(linear[:, :SPAN], low)

    def pass_on(g):
        @pl.when(stage > 0)
        def _():
            hop(g).wait_recv()

        state = came[g]
        goes[g] = apply(whole[g], state, jump[g])

        @pl.when(stage < outer - 1)
        def _():
            hop(g).start()

    def descend(g):
        state = came[g]
        for c in range(chips):
            start[g, c] = state
            if c < chips - 1:
                state = apply(inside[g, c], state, cross[g, c, SPAN:])
        for d in range(1, chips):
            down(g, d).start()
        chip_start[chip * groups + g] = start[g, chip]

    def spread(g):
        ms, _, _ = group(g)
        for d in range(1, chips):
            down_in(g, d).wait_recv()

        @pl.when(core == 1)
        def _():
            for m in ms:
                aside(chip_start, m).start()

        for m in ms:
            middle[m] = apply(first[m], chip_start[m], pair[m, 0, SPAN:])

        @pl.when(core == 0)
        def _():
            for m in ms:
                aside(middle, m).start()

    def read_terms(g):
        _, mine, theirs = group(g)
        hs = mine + theirs
        p, o = block_reads(*([ref[h] for h in hs] for ref in (q_ref, k_ref, solved, norms)), *masks())
        for j, h in enumerate(hs):
            solved[h] = jnp.concatenate([p[j], o[j]], 1)

    def put(hs, states):
        terms = [solved[h] for h in hs]
        states = [halves(x) for x in states]
        mixed = [x[:, SPAN:] + dot_halves(halves(x[:, :SPAN]), y) for x, y in zip(terms, states)]
        for h, x in zip(hs, mixed):
            o_ref[h] = x.astype(BF16)

    def finish(g):
        ms, mine, theirs = group(g)
        put(mine, [jnp.where(core == 0, chip_start[m], middle[m]) for m in ms])
        for m in ms:
            aside(middle, m).wait_recv()
        put(theirs, [side[m] for m in ms])

    ahead = jnp.minimum(groups, 2 + stage)
    busy = stage < 5 * outer // 8
    late = jnp.where(stage < outer // 4, groups + ahead, jnp.where(busy, groups, 0))
    below_at = jnp.maximum(late, ahead)

    def step(i, carry):
        def at(delay, do):
            @pl.when((i >= delay) & (i < delay + groups))
            def _():
                do(i - delay)

        at(0, prepare)
        at(1, compose)
        at(2, compose_chips)
        at(ahead, pass_on)
        at(late, read_terms)
        at(below_at, descend)
        at(below_at + 1, spread)
        at(below_at + 2, finish)
        return carry

    lax.fori_loop(0, groups + below_at + 2, step, 0)

    def drain(m, carry):
        give(m).wait_send()
        aside(middle, m).wait_send()
        return carry

    lax.fori_loop(0, owned, drain, 0)

    def drain_chain(g, carry):
        for d in range(1, chips):
            across(g, d).wait_send()
            down(g, d).wait_send()

        @pl.when(stage < outer - 1)
        def _():
            hop(g).wait_send()

        return carry

    lax.fori_loop(0, groups, drain_chain, 0)


def shards(outer, inner, query, keys, value, beta):
    tokens, heads, width = query.shape
    major = [jnp.transpose(x, (1, 0, 2)) for x in (query, keys, value)]
    gates = jnp.transpose(beta.astype(F32), (1, 0)).reshape(heads, 1, tokens)
    half, chips = heads // 2, inner // 2
    groups = half // chips
    vmem = pl.BlockSpec(memory_space=pltpu.VMEM)
    mixed = pl.pallas_call(
        functools.partial(kernel, outer, inner),
        out_shape=jax.ShapeDtypeStruct((heads, tokens, width), BF16),
        in_specs=[vmem] * 4,
        out_specs=vmem,
        scratch_shapes=[
            pltpu.VMEM((half, 2, 2 * width, width), F32),
            pltpu.VMEM((half, 2 * width, width), F32),
            pltpu.VMEM((heads, tokens, 2 * width), F32),
            pltpu.VMEM((heads, 1, tokens), F32),
            pltpu.VMEM((half, width, 2 * width), BF16),
            pltpu.VMEM((half, 2 * width, width), F32),
            pltpu.VMEM((groups, chips, 2 * width, width), F32),
            pltpu.VMEM((groups, width, 2 * width), BF16),
            pltpu.VMEM((groups, width, width), F32),
            pltpu.VMEM((groups, chips - 1, width, 2 * width), BF16),
            pltpu.VMEM((groups, width, width), F32),
            pltpu.VMEM((groups, width, width), F32),
            pltpu.VMEM((groups, chips, width, width), F32),
            *[pltpu.VMEM((half, width, width), F32)] * 3,
            pltpu.VMEM((SPAN, (BASE - 1) * SPAN), BF16),
            *[pltpu.SemaphoreType.DMA((half,))] * 4,
            *[pltpu.SemaphoreType.DMA((groups * (chips - 1),))] * 4,
            *[pltpu.SemaphoreType.DMA((groups,))] * 2,
        ],
        compiler_params=pltpu.CompilerParams(
            collective_id=0, has_side_effects=True, vmem_limit_bytes=40 * 2**20
        ),
        cost_estimate=pl.CostEstimate(flops=heads * 60 * 2 * 128**3, bytes_accessed=2**22, transcendentals=0),
    )(*major, gates)
    return jnp.transpose(mixed, (1, 0, 2))


def solution(mesh):
    placed = P(("outer", "inner"), None, None)
    return jax.shard_map(
        functools.partial(shards, mesh.shape["outer"], mesh.shape["inner"]),
        mesh=mesh,
        in_specs=(placed, placed, placed, P(("outer", "inner"), None)),
        out_specs=placed,
        check_vma=False,
    )
```

```python
import functools

import jax
import jax.numpy as jnp
from jax import lax
from jax.experimental import pallas as pl
from jax.experimental.pallas import tpu as pltpu
from jax.sharding import PartitionSpec as P

SPAN = 128
BASE = 16
PARTS = 2
F32 = jnp.float32
BF16 = jnp.bfloat16


def halves(x):
    high = x.astype(BF16)
    return high, (x - high.astype(F32)).astype(BF16)


def dot(a, b):
    return jnp.dot(a, b, preferred_element_type=F32)


def dot_halves(a, b):
    (ah, al), (bh, bl) = a, b
    return dot(jnp.concatenate([ah, al], 1), jnp.concatenate([bh, bh], 0)) + dot(ah, bl)


def dot_exact(a, b):
    ah, al = a
    return dot(jnp.concatenate([ah, al], 1), jnp.concatenate([b, b], 0))


def odd_rows(x, size):
    return jnp.concatenate([x[at : at + size] for at in range(size, SPAN, 2 * size)], 0)


def below(x, size):
    shape = (SPAN // 2, SPAN)
    block = lax.broadcasted_iota(jnp.int32, shape, 0) // size
    return jnp.where(lax.broadcasted_iota(jnp.int32, shape, 1) // size == 2 * block, odd_rows(x, size), jnp.zeros((), x.dtype))


def spaced(x, size):
    zeros = jnp.zeros((size, x.shape[1]), x.dtype)
    return jnp.concatenate([y for at in range(0, SPAN // 2, size) for y in (zeros, x[at : at + size])], 0)


def minus_odd_rows(x, change, size):
    out = []
    for at in range(0, SPAN // 2, size):
        out += [x[2 * at : 2 * at + size], x[2 * at + size : 2 * at + 2 * size] - change[at : at + size]]
    return jnp.concatenate(out, 0)


def diagonal_inverses(lower, pick):
    count = len(lower)
    row, lane = (lax.broadcasted_iota(jnp.int32, (BASE, SPAN), axis) for axis in (0, 1))
    here = [lane // BASE == k for k in range(SPAN // BASE)]
    beside = [sum(jnp.where(here[k], x[k * BASE : (k + 1) * BASE], 0.0) for k in range(SPAN // BASE)) for x in lower]
    split = [halves(x) for x in beside]
    spread = dot(jnp.concatenate([x for x, _ in split] + [x for _, x in split], 0), pick[...])
    spread = spread[: count * BASE] + spread[count * BASE :]
    found = [jnp.where(lane % BASE == row, 1.0, 0.0)] * count
    for c in range(BASE - 1):
        for i in range(count):
            factor = spread[i * BASE : (i + 1) * BASE, c * SPAN : (c + 1) * SPAN]
            found[i] = found[i] - factor * found[i][c : c + 1]
    return [jnp.concatenate([jnp.where(x, y, 0.0) for x in here], 0) for y in found]


def block_map(keys, value, brow, rows, cols, pick):
    eye = rows == cols
    width = keys[0].shape[1]
    count = range(len(keys))
    gram = [lax.dot_general(x, x, (((1,), (1,)), ((), ())), preferred_element_type=F32) for x in keys]
    kf = [x.astype(F32) for x in keys]
    krow = [lax.rsqrt(jnp.sum(jnp.where(eye, x, 0.0), axis=0, keepdims=True) + 1e-6) for x in gram]
    kcol = [lax.rsqrt(jnp.sum(x * x, axis=1, keepdims=True) + 1e-6) for x in kf]
    bcol = [jnp.sum(jnp.where(eye, x, 0.0), axis=1, keepdims=True) for x in brow]
    lower = [jnp.where(rows > cols, gram[i] * (bcol[i] * kcol[i]) * krow[i], 0.0) for i in count]
    inverse = diagonal_inverses(lower, pick)
    split = [halves(x) for x in lower]
    size = BASE
    while size < SPAN:
        inv = [halves(x) for x in inverse]
        part = [tuple(below(x, size) for x in y) for y in split]
        inner = [halves(dot_halves(part[i], inv[i])) for i in count]
        inner = [tuple(spaced(x, size) for x in y) for y in inner]
        change = [dot_halves(tuple(odd_rows(x, size) for x in inv[i]), inner[i]) for i in count]
        inverse = [minus_odd_rows(inverse[i], change[i], size) for i in count]
        size *= 2
    for_keys = [halves(inverse[i] * (brow[i] * krow[i])) for i in count]
    for_value = [halves(inverse[i] * brow[i]) for i in count]
    weights = [dot_exact(for_keys[i], keys[i]) for i in count]
    updates = [dot_exact(for_value[i], value[i]) for i in count]
    solved = [jnp.concatenate([weights[i], updates[i]], 1) for i in count]
    scaled = [halves(solved[i] * kcol[i]) for i in count]
    turned = [jnp.transpose(x) for x in keys]
    written = [dot(jnp.concatenate([turned[i]] * 2, 1), jnp.concatenate(scaled[i], 0)) for i in count]
    trans = [jnp.where(eye, 1.0, 0.0) - x[:, :width] for x in written]
    return trans, [x[:, width:] for x in written], solved, krow


def block_reads(query, keys, solved, krow, rows, cols):
    width = keys[0].shape[1]
    count = range(len(keys))
    raw = [
        lax.dot_general(q, k, (((1,), (1,)), ((), ())), preferred_element_type=F32) for q, k in zip(query, keys)
    ]
    qf = [x.astype(F32) for x in query]
    qcol = [lax.rsqrt(jnp.sum(x * x, axis=1, keepdims=True) + 1e-6) for x in qf]
    scores = [halves(jnp.where(rows >= cols, raw[i] * qcol[i] * krow[i], 0.0)) for i in count]
    solved = [halves(x) for x in solved]
    seen = [dot_halves(scores[i], solved[i]) for i in count]
    return [qf[i] * qcol[i] - seen[i][:, :width] for i in count], [x[:, width:] for x in seen]


def kernel(
    outer, inner, q_ref, k_ref, v_ref, b_ref, o_ref,
    pair, outgoing, solved, norms, first, chip_map, cross, whole, jump, inside, came, goes, start, chip_start, middle, side, pick,
    ab_send, ab_recv, side_send, side_recv, cross_send, cross_recv, down_send, down_recv, chain_send, chain_recv,
):
    heads = q_ref.shape[0]
    owned = heads // 2
    chips = inner // 2
    groups = owned // chips
    total = outer * inner
    stage, place_in = lax.axis_index("outer"), lax.axis_index("inner")
    core, chip = lax.rem(place_in, 2), place_in // 2
    after, before = lax.rem(stage + 1, outer), lax.rem(stage + outer - 1, outer)
    sibling = (stage, place_in + 1 - 2 * core)

    def turned(d):
        return lax.rem(chip + d, chips)

    def beside(other):
        return (stage, other * 2 + core)

    barrier = pltpu.get_barrier_semaphore()
    met = [(after, place_in), (before, place_in), sibling] + [beside(turned(d)) for d in range(1, chips)]
    for other in met:
        pl.semaphore_signal(barrier, inc=1, device_id=other, device_id_type=pl.DeviceIdType.MESH)
    pl.semaphore_wait(barrier, len(met))

    def send(src, dst, send_sem, recv_sem, to):
        return pltpu.make_async_remote_copy(
            src_ref=src,
            dst_ref=dst,
            send_sem=send_sem,
            recv_sem=recv_sem,
            device_id=to,
            device_id_type=pl.DeviceIdType.MESH,
        )

    def give(m):
        return send(outgoing.at[m], pair.at[m, core], ab_send.at[m], ab_recv.at[m], sibling)

    def across(g, d):
        other, at = turned(d), g * (chips - 1) + d - 1
        return send(chip_map.at[other * groups + g], cross.at[g, chip], cross_send.at[at], cross_recv.at[at], beside(other))

    def across_in(g, d):
        other, at = turned(chips - d), g * (chips - 1) + d - 1
        return send(chip_map.at[g], cross.at[g, other], cross_send.at[at], cross_recv.at[at], beside(other))

    def part(p):
        return pl.ds(p * SPAN // PARTS, SPAN // PARTS)

    def hop(g, p):
        at = g * PARTS + p
        return send(goes.at[g, part(p)], came.at[g, part(p)], chain_send.at[at], chain_recv.at[at], (after, place_in))

    def down(g, d):
        other, at = turned(d), g * (chips - 1) + d - 1
        return send(start.at[g, other], chip_start.at[chip * groups + g], down_send.at[at], down_recv.at[at], beside(other))

    def down_in(g, d):
        other, at = turned(chips - d), g * (chips - 1) + d - 1
        return send(start.at[g, other], chip_start.at[other * groups + g], down_send.at[at], down_recv.at[at], beside(other))

    def aside(src, m):
        return send(src.at[m], side.at[m], side_send.at[m], side_recv.at[m], sibling)

    @pl.when(stage == 0)
    def _():
        came[...] = jnp.zeros_like(came)

    def masks():
        return [lax.broadcasted_iota(jnp.int32, (SPAN, SPAN), axis) for axis in (0, 1)]

    row, lane = masks()
    for c in range(BASE - 1):
        pick[:, c * SPAN : (c + 1) * SPAN] = jnp.where(row == lane // BASE * BASE + c, 1.0, 0.0).astype(BF16)

    def group(g):
        ms = [c * groups + g for c in range(chips)]
        return ms, [core * owned + m for m in ms], [(1 - core) * owned + m for m in ms]

    def prepare(g):
        ms, mine, theirs = group(g)
        hs = mine + theirs
        a, b, wu, krow = block_map(*([ref[h] for h in hs] for ref in (k_ref, v_ref, b_ref)), *masks(), pick)
        for j, h in enumerate(hs):
            solved[h] = wu[j]
            norms[h] = krow[j]
        for j, m in enumerate(ms):
            outgoing[m, :SPAN] = a[chips + j]
            outgoing[m, SPAN:] = b[chips + j]
        for m in ms:
            give(m).start()
        for j, m in enumerate(ms):
            pair[m, core, :SPAN] = a[j]
            pair[m, core, SPAN:] = b[j]

    def compose(g):
        ms, _, _ = group(g)
        for m in ms:
            send(outgoing.at[m], pair.at[m, 1 - core], ab_send.at[m], ab_recv.at[m], sibling).wait_recv()
        early = [halves(jnp.concatenate([pair[m, 0, :SPAN], pair[m, 0, SPAN:]], 1)) for m in ms]
        late = [halves(pair[m, 1, :SPAN]) for m in ms]
        both = [dot_halves(x, y) for x, y in zip(late, early)]
        for j, m in enumerate(ms):
            chip_map[m, :SPAN] = both[j][:, :SPAN]
            chip_map[m, SPAN:] = both[j][:, SPAN:] + pair[m, 1, SPAN:]
        for d in range(1, chips):
            across(g, d).start()
        for j, m in enumerate(ms):
            first[m] = jnp.concatenate([x[:, :SPAN] for x in early[j]], 1)
        cross[g, chip] = chip_map[chip * groups + g]

    def compose_chips(g):
        for d in range(1, chips):
            across_in(g, d).wait_recv()
        both = jnp.concatenate([cross[g, 0, :SPAN], cross[g, 0, SPAN:]], 1)
        for c in range(1, chips):
            split = halves(both)
            if c == 1:
                inside[g, 0] = jnp.concatenate([x[:, :SPAN] for x in split], 1)
            late = halves(cross[g, c, :SPAN])
            if c < chips - 1:
                inside[g, c] = jnp.concatenate(late, 1)
            moved = dot_halves(late, split)
            both = jnp.concatenate([moved[:, :SPAN], moved[:, SPAN:] + cross[g, c, SPAN:]], 1)
        whole[g] = jnp.concatenate(halves(jnp.transpose(both[:, :SPAN])), 0)
        jump[g] = jnp.transpose(both[:, SPAN:])

    def apply(linear, state, constant):
        high, low = halves(state)
        return constant + dot(linear, jnp.concatenate([high, high], 0)) + dot(linear[:, :SPAN], low)

    def pass_on(g):
        for p in range(PARTS):
            @pl.when(stage > 0)
            def _():
                hop(g, p).wait_recv()

            @pl.when(stage < outer - 1)
            def _():
                high, low = whole[g, :SPAN], whole[g, SPAN:]
                state = halves(came[g, part(p)])
                goes[g, part(p)] = jump[g, part(p)] + dot_exact(state, high) + dot(state[0], low)
                hop(g, p).start()

    def descend(g):
        state = jnp.transpose(came[g])
        for c in range(chips):
            start[g, c] = state
            if c < chips - 1:
                state = apply(inside[g, c], state, cross[g, c, SPAN:])
        for d in range(1, chips):
            down(g, d).start()
        chip_start[chip * groups + g] = start[g, chip]

    def spread(g):
        ms, _, _ = group(g)
        for d in range(1, chips):
            down_in(g, d).wait_recv()

        @pl.when(core == 1)
        def _():
            for m in ms:
                aside(chip_start, m).start()

        for m in ms:
            middle[m] = apply(first[m], chip_start[m], pair[m, 0, SPAN:])

        @pl.when(core == 0)
        def _():
            for m in ms:
                aside(middle, m).start()

    def read_terms(g):
        _, mine, theirs = group(g)
        hs = mine + theirs
        p, o = block_reads(*([ref[h] for h in hs] for ref in (q_ref, k_ref, solved, norms)), *masks())
        for j, h in enumerate(hs):
            solved[h] = jnp.concatenate([p[j], o[j]], 1)

    def put(hs, states):
        terms = [solved[h] for h in hs]
        states = [halves(x) for x in states]
        mixed = [x[:, SPAN:] + dot_halves(halves(x[:, :SPAN]), y) for x, y in zip(terms, states)]
        for h, x in zip(hs, mixed):
            o_ref[h] = x.astype(BF16)

    def finish(g):
        ms, mine, theirs = group(g)
        put(mine, [jnp.where(core == 0, chip_start[m], middle[m]) for m in ms])
        for m in ms:
            aside(middle, m).wait_recv()
        put(theirs, [side[m] for m in ms])

    ahead = jnp.minimum(groups, 2 + stage)
    busy = stage < 5 * outer // 8
    late = jnp.where(stage < outer // 4, groups + ahead, jnp.where(busy, groups, 0))
    below_at = jnp.maximum(late, ahead)

    def step(i, carry):
        def at(delay, do):
            @pl.when((i >= delay) & (i < delay + groups))
            def _():
                do(i - delay)

        at(0, prepare)
        at(1, compose)
        at(2, compose_chips)
        at(below_at + 2, finish)
        at(below_at + 1, spread)
        at(ahead, pass_on)
        at(below_at, descend)
        at(late, read_terms)
        return carry

    lax.fori_loop(0, groups + below_at + 2, step, 0)

    def drain(m, carry):
        give(m).wait_send()
        aside(middle, m).wait_send()
        return carry

    lax.fori_loop(0, owned, drain, 0)

    def drain_chain(g, carry):
        for d in range(1, chips):
            across(g, d).wait_send()
            down(g, d).wait_send()

        @pl.when(stage < outer - 1)
        def _():
            for p in range(PARTS):
                hop(g, p).wait_send()

        return carry

    lax.fori_loop(0, groups, drain_chain, 0)


def shards(outer, inner, query, keys, value, beta):
    tokens, heads, width = query.shape
    major = [jnp.transpose(x, (1, 0, 2)) for x in (query, keys, value)]
    gates = jnp.transpose(beta.astype(F32), (1, 0)).reshape(heads, 1, tokens)
    half, chips = heads // 2, inner // 2
    groups = half // chips
    vmem = pl.BlockSpec(memory_space=pltpu.VMEM)
    mixed = pl.pallas_call(
        functools.partial(kernel, outer, inner),
        out_shape=jax.ShapeDtypeStruct((heads, tokens, width), BF16),
        in_specs=[vmem] * 4,
        out_specs=vmem,
        scratch_shapes=[
            pltpu.VMEM((half, 2, 2 * width, width), F32),
            pltpu.VMEM((half, 2 * width, width), F32),
            pltpu.VMEM((heads, tokens, 2 * width), F32),
            pltpu.VMEM((heads, 1, tokens), F32),
            pltpu.VMEM((half, width, 2 * width), BF16),
            pltpu.VMEM((half, 2 * width, width), F32),
            pltpu.VMEM((groups, chips, 2 * width, width), F32),
            pltpu.VMEM((groups, 2 * width, width), BF16),
            pltpu.VMEM((groups, width, width), F32),
            pltpu.VMEM((groups, chips - 1, width, 2 * width), BF16),
            pltpu.VMEM((groups, width, width), F32),
            pltpu.VMEM((groups, width, width), F32),
            pltpu.VMEM((groups, chips, width, width), F32),
            *[pltpu.VMEM((half, width, width), F32)] * 3,
            pltpu.VMEM((SPAN, (BASE - 1) * SPAN), BF16),
            *[pltpu.SemaphoreType.DMA((half,))] * 4,
            *[pltpu.SemaphoreType.DMA((groups * (chips - 1),))] * 4,
            *[pltpu.SemaphoreType.DMA((groups * PARTS,))] * 2,
        ],
        compiler_params=pltpu.CompilerParams(
            collective_id=0, has_side_effects=True, vmem_limit_bytes=40 * 2**20
        ),
        cost_estimate=pl.CostEstimate(flops=heads * 60 * 2 * 128**3, bytes_accessed=2**22, transcendentals=0),
    )(*major, gates)
    return jnp.transpose(mixed, (1, 0, 2))


def solution(mesh):
    placed = P(("outer", "inner"), None, None)
    return jax.shard_map(
        functools.partial(shards, mesh.shape["outer"], mesh.shape["inner"]),
        mesh=mesh,
        in_specs=(placed, placed, placed, P(("outer", "inner"), None)),
        out_specs=placed,
        check_vma=False,
    )
```

```python
import functools

import jax
import jax.numpy as jnp
from jax import lax
from jax.experimental import pallas as pl
from jax.experimental.pallas import tpu as pltpu
from jax.sharding import PartitionSpec as P

SPAN = 128
BASE = 16
F32 = jnp.float32
BF16 = jnp.bfloat16


def halves(x):
    high = x.astype(BF16)
    return high, (x - high.astype(F32)).astype(BF16)


def dot(a, b):
    return jnp.dot(a, b, preferred_element_type=F32)


def dot_halves(a, b):
    (ah, al), (bh, bl) = a, b
    return dot(jnp.concatenate([ah, al], 1), jnp.concatenate([bh, bh], 0)) + dot(ah, bl)


def dot_exact(a, b):
    ah, al = a
    return dot(jnp.concatenate([ah, al], 1), jnp.concatenate([b, b], 0))


def odd_rows(x, size):
    return jnp.concatenate([x[at : at + size] for at in range(size, SPAN, 2 * size)], 0)


def below(x, size):
    shape = (SPAN // 2, SPAN)
    block = lax.broadcasted_iota(jnp.int32, shape, 0) // size
    return jnp.where(lax.broadcasted_iota(jnp.int32, shape, 1) // size == 2 * block, odd_rows(x, size), jnp.zeros((), x.dtype))


def spaced(x, size):
    zeros = jnp.zeros((size, x.shape[1]), x.dtype)
    return jnp.concatenate([y for at in range(0, SPAN // 2, size) for y in (zeros, x[at : at + size])], 0)


def minus_odd_rows(x, change, size):
    out = []
    for at in range(0, SPAN // 2, size):
        out += [x[2 * at : 2 * at + size], x[2 * at + size : 2 * at + 2 * size] - change[at : at + size]]
    return jnp.concatenate(out, 0)


def diagonal_inverses(lower, pick):
    count = len(lower)
    row, lane = (lax.broadcasted_iota(jnp.int32, (BASE, SPAN), axis) for axis in (0, 1))
    here = [lane // BASE == k for k in range(SPAN // BASE)]
    beside = [sum(jnp.where(here[k], x[k * BASE : (k + 1) * BASE], 0.0) for k in range(SPAN // BASE)) for x in lower]
    split = [halves(x) for x in beside]
    spread = dot(jnp.concatenate([x for x, _ in split] + [x for _, x in split], 0), pick[...])
    spread = spread[: count * BASE] + spread[count * BASE :]
    found = [jnp.where(lane % BASE == row, 1.0, 0.0)] * count
    for c in range(BASE - 1):
        for i in range(count):
            factor = spread[i * BASE : (i + 1) * BASE, c * SPAN : (c + 1) * SPAN]
            found[i] = found[i] - factor * found[i][c : c + 1]
    return [jnp.concatenate([jnp.where(x, y, 0.0) for x in here], 0) for y in found]


def block_map(keys, value, brow, rows, cols, pick):
    eye = rows == cols
    width = keys[0].shape[1]
    count = range(len(keys))
    ones = jnp.where(eye, 1.0, 0.0).astype(BF16)
    both = [
        lax.dot_general(
            jnp.concatenate([x, ones], 0), x, (((1,), (1,)), ((), ())), preferred_element_type=F32
        )
        for x in keys
    ]
    gram, turned = [x[:SPAN] for x in both], [x[SPAN:].astype(BF16) for x in both]
    kf = [x.astype(F32) for x in keys]
    krow = [lax.rsqrt(jnp.sum(jnp.where(eye, x, 0.0), axis=0, keepdims=True) + 1e-6) for x in gram]
    kcol = [lax.rsqrt(jnp.sum(x * x, axis=1, keepdims=True) + 1e-6) for x in kf]
    bcol = [jnp.sum(jnp.where(eye, x, 0.0), axis=1, keepdims=True) for x in brow]
    lower = [jnp.where(rows > cols, gram[i] * (bcol[i] * kcol[i]) * krow[i], 0.0) for i in count]
    inverse = diagonal_inverses(lower, pick)
    size = BASE
    while size < SPAN:
        inv = [halves(x) for x in inverse]
        part = [halves(below(x, size)) for x in lower]
        inner = [halves(dot_halves(part[i], inv[i])) for i in count]
        inner = [tuple(spaced(x, size) for x in y) for y in inner]
        change = [dot_halves(tuple(odd_rows(x, size) for x in inv[i]), inner[i]) for i in count]
        inverse = [minus_odd_rows(inverse[i], change[i], size) for i in count]
        size *= 2
    for_keys = [halves(inverse[i] * (brow[i] * krow[i])) for i in count]
    for_value = [halves(inverse[i] * brow[i]) for i in count]
    weights = [dot_exact(for_keys[i], keys[i]) for i in count]
    updates = [dot_exact(for_value[i], value[i]) for i in count]
    solved = [jnp.concatenate([weights[i], updates[i]], 1) for i in count]
    scaled = [halves(solved[i] * kcol[i]) for i in count]
    written = [dot(jnp.concatenate([turned[i]] * 2, 1), jnp.concatenate(scaled[i], 0)) for i in count]
    trans = [jnp.where(eye, 1.0, 0.0) - x[:, :width] for x in written]
    return trans, [x[:, width:] for x in written], solved, krow


def block_reads(query, keys, solved, krow, rows, cols):
    width = keys[0].shape[1]
    count = range(len(keys))
    raw = [
        lax.dot_general(q, k, (((1,), (1,)), ((), ())), preferred_element_type=F32) for q, k in zip(query, keys)
    ]
    qf = [x.astype(F32) for x in query]
    qcol = [lax.rsqrt(jnp.sum(x * x, axis=1, keepdims=True) + 1e-6) for x in qf]
    scores = [halves(jnp.where(rows >= cols, raw[i] * qcol[i] * krow[i], 0.0)) for i in count]
    solved = [halves(x) for x in solved]
    seen = [dot_halves(scores[i], solved[i]) for i in count]
    return [qf[i] * qcol[i] - seen[i][:, :width] for i in count], [x[:, width:] for x in seen]


def kernel(
    outer, inner, q_ref, k_ref, v_ref, b_ref, o_ref,
    pair, outgoing, solved, norms, first, chip_map, cross, whole, jump, inside, came, goes, start, chip_start, middle, side, pick,
    ab_send, ab_recv, side_send, side_recv, cross_send, cross_recv, down_send, down_recv, chain_send, chain_recv,
):
    heads = q_ref.shape[0]
    owned = heads // 2
    chips = inner // 2
    groups = owned // chips
    total = outer * inner
    stage, place_in = lax.axis_index("outer"), lax.axis_index("inner")
    core, chip = lax.rem(place_in, 2), place_in // 2
    after, before = lax.rem(stage + 1, outer), lax.rem(stage + outer - 1, outer)
    sibling = (stage, place_in + 1 - 2 * core)

    def turned(d):
        return lax.rem(chip + d, chips)

    def beside(other):
        return (stage, other * 2 + core)

    barrier = pltpu.get_barrier_semaphore()
    met = [(after, place_in), (before, place_in), sibling] + [beside(turned(d)) for d in range(1, chips)]
    for other in met:
        pl.semaphore_signal(barrier, inc=1, device_id=other, device_id_type=pl.DeviceIdType.MESH)
    pl.semaphore_wait(barrier, len(met))

    def send(src, dst, send_sem, recv_sem, to):
        return pltpu.make_async_remote_copy(
            src_ref=src,
            dst_ref=dst,
            send_sem=send_sem,
            recv_sem=recv_sem,
            device_id=to,
            device_id_type=pl.DeviceIdType.MESH,
        )

    def give(m):
        return send(outgoing.at[m], pair.at[m, core], ab_send.at[m], ab_recv.at[m], sibling)

    def across(g, d):
        other, at = turned(d), g * (chips - 1) + d - 1
        return send(chip_map.at[other * groups + g], cross.at[g, chip], cross_send.at[at], cross_recv.at[at], beside(other))

    def across_in(g, d):
        other, at = turned(chips - d), g * (chips - 1) + d - 1
        return send(chip_map.at[g], cross.at[g, other], cross_send.at[at], cross_recv.at[at], beside(other))

    def hop(g):
        return send(goes.at[g], came.at[g], chain_send.at[g], chain_recv.at[g], (after, place_in))

    def down(g, d):
        other, at = turned(d), g * (chips - 1) + d - 1
        return send(start.at[g, other], chip_start.at[chip * groups + g], down_send.at[at], down_recv.at[at], beside(other))

    def down_in(g, d):
        other, at = turned(chips - d), g * (chips - 1) + d - 1
        return send(start.at[g, other], chip_start.at[other * groups + g], down_send.at[at], down_recv.at[at], beside(other))

    def aside(src, m):
        return send(src.at[m], side.at[m], side_send.at[m], side_recv.at[m], sibling)

    @pl.when(stage == 0)
    def _():
        came[...] = jnp.zeros_like(came)

    def masks():
        return [lax.broadcasted_iota(jnp.int32, (SPAN, SPAN), axis) for axis in (0, 1)]

    row, lane = masks()
    for c in range(BASE - 1):
        pick[:, c * SPAN : (c + 1) * SPAN] = jnp.where(row == lane // BASE * BASE + c, 1.0, 0.0).astype(BF16)

    def group(g):
        ms = [c * groups + g for c in range(chips)]
        return ms, [core * owned + m for m in ms], [(1 - core) * owned + m for m in ms]

    def prepare(g):
        ms, mine, theirs = group(g)
        hs = mine + theirs
        a, b, wu, krow = block_map(*([ref[h] for h in hs] for ref in (k_ref, v_ref, b_ref)), *masks(), pick)
        for j, h in enumerate(hs):
            solved[h] = wu[j]
            norms[h] = krow[j]
        for j, m in enumerate(ms):
            outgoing[m, :SPAN] = a[chips + j]
            outgoing[m, SPAN:] = b[chips + j]
        for m in ms:
            give(m).start()
        for j, m in enumerate(ms):
            pair[m, core, :SPAN] = a[j]
            pair[m, core, SPAN:] = b[j]

    def compose(g):
        ms, _, _ = group(g)
        for m in ms:
            send(outgoing.at[m], pair.at[m, 1 - core], ab_send.at[m], ab_recv.at[m], sibling).wait_recv()
        early = [halves(jnp.concatenate([pair[m, 0, :SPAN], pair[m, 0, SPAN:]], 1)) for m in ms]
        late = [halves(pair[m, 1, :SPAN]) for m in ms]
        both = [dot_halves(x, y) for x, y in zip(late, early)]
        for j, m in enumerate(ms):
            chip_map[m, :SPAN] = both[j][:, :SPAN]
            chip_map[m, SPAN:] = both[j][:, SPAN:] + pair[m, 1, SPAN:]
        for d in range(1, chips):
            across(g, d).start()
        for j, m in enumerate(ms):
            first[m] = jnp.concatenate([x[:, :SPAN] for x in early[j]], 1)
        cross[g, chip] = chip_map[chip * groups + g]

    def compose_chips(g):
        for d in range(1, chips):
            across_in(g, d).wait_recv()
        both = jnp.concatenate([cross[g, 0, :SPAN], cross[g, 0, SPAN:]], 1)
        for c in range(1, chips):
            split = halves(both)
            if c == 1:
                inside[g, 0] = jnp.concatenate([x[:, :SPAN] for x in split], 1)
            late = halves(cross[g, c, :SPAN])
            if c < chips - 1:
                inside[g, c] = jnp.concatenate(late, 1)
            moved = dot_halves(late, split)
            both = jnp.concatenate([moved[:, :SPAN], moved[:, SPAN:] + cross[g, c, SPAN:]], 1)
        whole[g] = jnp.concatenate(halves(both[:, :SPAN]), 1)
        jump[g] = both[:, SPAN:]

    def apply(linear, state, constant):
        high, low = halves(state)
        return constant + dot(linear, jnp.concatenate([high, high], 0)) + dot(linear[:, :SPAN], low)

    def pass_on(g):
        @pl.when(stage > 0)
        def _():
            hop(g).wait_recv()

        @pl.when(stage < outer - 1)
        def _():
            goes[g] = apply(whole[g], came[g], jump[g])
            hop(g).start()

    def descend(g):
        state = came[g]
        for c in range(chips):
            start[g, c] = state
            if c < chips - 1:
                state = apply(inside[g, c], state, cross[g, c, SPAN:])
        for d in range(1, chips):
            down(g, d).start()
        chip_start[chip * groups + g] = start[g, chip]

    def spread(g):
        ms, _, _ = group(g)
        for d in range(1, chips):
            down_in(g, d).wait_recv()

        @pl.when(core == 1)
        def _():
            for m in ms:
                aside(chip_start, m).start()

        for m in ms:
            middle[m] = apply(first[m], chip_start[m], pair[m, 0, SPAN:])

        @pl.when(core == 0)
        def _():
            for m in ms:
                aside(middle, m).start()

    def read_terms(g):
        _, mine, theirs = group(g)
        hs = mine + theirs
        p, o = block_reads(*([ref[h] for h in hs] for ref in (q_ref, k_ref, solved, norms)), *masks())
        for j, h in enumerate(hs):
            solved[h] = jnp.concatenate([p[j], o[j]], 1)

    def put(hs, states):
        terms = [solved[h] for h in hs]
        states = [halves(x) for x in states]
        mixed = [x[:, SPAN:] + dot_halves(halves(x[:, :SPAN]), y) for x, y in zip(terms, states)]
        for h, x in zip(hs, mixed):
            o_ref[h] = x.astype(BF16)

    def finish(g):
        ms, mine, theirs = group(g)
        put(mine, [jnp.where(core == 0, chip_start[m], middle[m]) for m in ms])
        for m in ms:
            aside(middle, m).wait_recv()
        put(theirs, [side[m] for m in ms])

    ahead = jnp.minimum(groups, 2 + stage)
    busy = stage < 5 * outer // 8
    late = jnp.where(stage < outer // 4, groups + ahead, jnp.where(busy, groups, 0))
    below_at = jnp.maximum(late, ahead)

    def step(i, carry):
        def at(delay, do):
            @pl.when((i >= delay) & (i < delay + groups))
            def _():
                do(i - delay)

        at(0, prepare)
        at(1, compose)
        at(2, compose_chips)
        at(ahead, pass_on)
        at(late, read_terms)
        at(below_at, descend)
        at(below_at + 1, spread)
        at(below_at + 2, finish)
        return carry

    lax.fori_loop(0, groups + below_at + 2, step, 0)

    def drain(m, carry):
        give(m).wait_send()
        aside(middle, m).wait_send()
        return carry

    lax.fori_loop(0, owned, drain, 0)

    def drain_chain(g, carry):
        for d in range(1, chips):
            across(g, d).wait_send()
            down(g, d).wait_send()

        @pl.when(stage < outer - 1)
        def _():
            hop(g).wait_send()

        return carry

    lax.fori_loop(0, groups, drain_chain, 0)


def shards(outer, inner, query, keys, value, beta):
    tokens, heads, width = query.shape
    major = [jnp.transpose(x, (1, 0, 2)) for x in (query, keys, value)]
    gates = jnp.transpose(beta.astype(F32), (1, 0)).reshape(heads, 1, tokens)
    half, chips = heads // 2, inner // 2
    groups = half // chips
    vmem = pl.BlockSpec(memory_space=pltpu.VMEM)
    mixed = pl.pallas_call(
        functools.partial(kernel, outer, inner),
        out_shape=jax.ShapeDtypeStruct((heads, tokens, width), BF16),
        in_specs=[vmem] * 4,
        out_specs=vmem,
        scratch_shapes=[
            pltpu.VMEM((half, 2, 2 * width, width), F32),
            pltpu.VMEM((half, 2 * width, width), F32),
            pltpu.VMEM((heads, tokens, 2 * width), F32),
            pltpu.VMEM((heads, 1, tokens), F32),
            pltpu.VMEM((half, width, 2 * width), BF16),
            pltpu.VMEM((half, 2 * width, width), F32),
            pltpu.VMEM((groups, chips, 2 * width, width), F32),
            pltpu.VMEM((groups, width, 2 * width), BF16),
            pltpu.VMEM((groups, width, width), F32),
            pltpu.VMEM((groups, chips - 1, width, 2 * width), BF16),
            pltpu.VMEM((groups, width, width), F32),
            pltpu.VMEM((groups, width, width), F32),
            pltpu.VMEM((groups, chips, width, width), F32),
            *[pltpu.VMEM((half, width, width), F32)] * 3,
            pltpu.VMEM((SPAN, (BASE - 1) * SPAN), BF16),
            *[pltpu.SemaphoreType.DMA((half,))] * 4,
            *[pltpu.SemaphoreType.DMA((groups * (chips - 1),))] * 4,
            *[pltpu.SemaphoreType.DMA((groups,))] * 2,
        ],
        compiler_params=pltpu.CompilerParams(
            collective_id=0, has_side_effects=True, vmem_limit_bytes=40 * 2**20
        ),
        cost_estimate=pl.CostEstimate(flops=heads * 60 * 2 * 128**3, bytes_accessed=2**22, transcendentals=0),
    )(*major, gates)
    return jnp.transpose(mixed, (1, 0, 2))


def solution(mesh):
    placed = P(("outer", "inner"), None, None)
    return jax.shard_map(
        functools.partial(shards, mesh.shape["outer"], mesh.shape["inner"]),
        mesh=mesh,
        in_specs=(placed, placed, placed, P(("outer", "inner"), None)),
        out_specs=placed,
        check_vma=False,
    )
```

```python
import functools

import jax
import jax.numpy as jnp
from jax import lax
from jax.experimental import pallas as pl
from jax.experimental.pallas import tpu as pltpu
from jax.sharding import PartitionSpec as P

SPAN = 128
BASE = 16
F32 = jnp.float32
BF16 = jnp.bfloat16


def halves(x):
    high = x.astype(BF16)
    return high, (x - high.astype(F32)).astype(BF16)


def dot(a, b):
    return jnp.dot(a, b, preferred_element_type=F32)


def dot_halves(a, b):
    (ah, al), (bh, bl) = a, b
    return dot(jnp.concatenate([ah, al], 1), jnp.concatenate([bh, bh], 0)) + dot(ah, bl)


def dot_exact(a, b):
    ah, al = a
    return dot(jnp.concatenate([ah, al], 1), jnp.concatenate([b, b], 0))


def odd_rows(x, size):
    return jnp.concatenate([x[at : at + size] for at in range(size, SPAN, 2 * size)], 0)


def below(x, size):
    shape = (SPAN // 2, SPAN)
    block = lax.broadcasted_iota(jnp.int32, shape, 0) // size
    return jnp.where(lax.broadcasted_iota(jnp.int32, shape, 1) // size == 2 * block, odd_rows(x, size), jnp.zeros((), x.dtype))


def spaced(x, size):
    zeros = jnp.zeros((size, x.shape[1]), x.dtype)
    return jnp.concatenate([y for at in range(0, SPAN // 2, size) for y in (zeros, x[at : at + size])], 0)


def minus_odd_rows(x, change, size):
    out = []
    for at in range(0, SPAN // 2, size):
        out += [x[2 * at : 2 * at + size], x[2 * at + size : 2 * at + 2 * size] - change[at : at + size]]
    return jnp.concatenate(out, 0)


def diagonal_inverses(lower, pick):
    count = len(lower)
    row, lane = (lax.broadcasted_iota(jnp.int32, (BASE, SPAN), axis) for axis in (0, 1))
    here = [lane // BASE == k for k in range(SPAN // BASE)]
    beside = [sum(jnp.where(here[k], x[k * BASE : (k + 1) * BASE], 0.0) for k in range(SPAN // BASE)) for x in lower]
    split = [halves(x) for x in beside]
    spread = dot(jnp.concatenate([x for x, _ in split] + [x for _, x in split], 0), pick[...])
    spread = spread[: count * BASE] + spread[count * BASE :]
    found = [jnp.where(lane % BASE == row, 1.0, 0.0)] * count
    for c in range(BASE - 1):
        for i in range(count):
            factor = spread[i * BASE : (i + 1) * BASE, c * SPAN : (c + 1) * SPAN]
            found[i] = found[i] - factor * found[i][c : c + 1]
    return [jnp.concatenate([jnp.where(x, y, 0.0) for x in here], 0) for y in found]


def block_map(keys, value, brow, rows, cols, pick):
    eye = rows == cols
    width = keys[0].shape[1]
    count = range(len(keys))
    ones = jnp.where(eye, 1.0, 0.0).astype(BF16)
    both = [
        lax.dot_general(
            jnp.concatenate([x, ones], 0), x, (((1,), (1,)), ((), ())), preferred_element_type=F32
        )
        for x in keys
    ]
    gram, turned = [x[:SPAN] for x in both], [x[SPAN:].astype(BF16) for x in both]
    kf = [x.astype(F32) for x in keys]
    krow = [lax.rsqrt(jnp.sum(jnp.where(eye, x, 0.0), axis=0, keepdims=True) + 1e-6) for x in gram]
    kcol = [lax.rsqrt(jnp.sum(x * x, axis=1, keepdims=True) + 1e-6) for x in kf]
    bcol = [jnp.sum(jnp.where(eye, x, 0.0), axis=1, keepdims=True) for x in brow]
    lower = [jnp.where(rows > cols, gram[i] * (bcol[i] * kcol[i]) * krow[i], 0.0) for i in count]
    inverse = diagonal_inverses(lower, pick)
    size = BASE
    while size < SPAN:
        inv = [halves(x) for x in inverse]
        part = [halves(below(x, size)) for x in lower]
        inner = [halves(dot_halves(part[i], inv[i])) for i in count]
        inner = [tuple(spaced(x, size) for x in y) for y in inner]
        change = [dot_halves(tuple(odd_rows(x, size) for x in inv[i]), inner[i]) for i in count]
        inverse = [minus_odd_rows(inverse[i], change[i], size) for i in count]
        size *= 2
    for_keys = [halves(inverse[i] * (brow[i] * krow[i])) for i in count]
    for_value = [halves(inverse[i] * brow[i]) for i in count]
    weights = [dot_exact(for_keys[i], keys[i]) for i in count]
    updates = [dot_exact(for_value[i], value[i]) for i in count]
    solved = [jnp.concatenate([weights[i], updates[i]], 1) for i in count]
    scaled = [halves(solved[i] * kcol[i]) for i in count]
    written = [dot(jnp.concatenate([turned[i]] * 2, 1), jnp.concatenate(scaled[i], 0)) for i in count]
    trans = [jnp.where(eye, 1.0, 0.0) - x[:, :width] for x in written]
    return trans, [x[:, width:] for x in written], solved, krow


def block_reads(query, keys, solved, krow, rows, cols):
    width = keys[0].shape[1]
    count = range(len(keys))
    raw = [
        lax.dot_general(q, k, (((1,), (1,)), ((), ())), preferred_element_type=F32) for q, k in zip(query, keys)
    ]
    qf = [x.astype(F32) for x in query]
    qcol = [lax.rsqrt(jnp.sum(x * x, axis=1, keepdims=True) + 1e-6) for x in qf]
    scores = [halves(jnp.where(rows >= cols, raw[i] * qcol[i] * krow[i], 0.0)) for i in count]
    solved = [halves(x) for x in solved]
    seen = [dot_halves(scores[i], solved[i]) for i in count]
    return [qf[i] * qcol[i] - seen[i][:, :width] for i in count], [x[:, width:] for x in seen]


def kernel(
    outer, inner, q_ref, k_ref, v_ref, b_ref, o_ref,
    pair, outgoing, solved, norms, first, chip_map, cross, whole, jump, inside, came, goes, start, chip_start, middle, side, pick,
    ab_send, ab_recv, side_send, side_recv, cross_send, cross_recv, down_send, down_recv, chain_send, chain_recv,
):
    heads = q_ref.shape[0]
    owned = heads // 2
    chips = inner // 2
    groups = owned // chips
    total = outer * inner
    stage, place_in = lax.axis_index("outer"), lax.axis_index("inner")
    core, chip = lax.rem(place_in, 2), place_in // 2
    after, before = lax.rem(stage + 1, outer), lax.rem(stage + outer - 1, outer)
    sibling = (stage, place_in + 1 - 2 * core)

    def turned(d):
        return lax.rem(chip + d, chips)

    def beside(other):
        return (stage, other * 2 + core)

    barrier = pltpu.get_barrier_semaphore()
    met = [(after, place_in), (before, place_in), sibling] + [beside(turned(d)) for d in range(1, chips)]
    for other in met:
        pl.semaphore_signal(barrier, inc=1, device_id=other, device_id_type=pl.DeviceIdType.MESH)
    pl.semaphore_wait(barrier, len(met))

    def send(src, dst, send_sem, recv_sem, to):
        return pltpu.make_async_remote_copy(
            src_ref=src,
            dst_ref=dst,
            send_sem=send_sem,
            recv_sem=recv_sem,
            device_id=to,
            device_id_type=pl.DeviceIdType.MESH,
        )

    def give(m):
        return send(outgoing.at[m], pair.at[m, core], ab_send.at[m], ab_recv.at[m], sibling)

    def across(g, d):
        other, at = turned(d), g * (chips - 1) + d - 1
        return send(chip_map.at[other * groups + g], cross.at[g, chip], cross_send.at[at], cross_recv.at[at], beside(other))

    def across_in(g, d):
        other, at = turned(chips - d), g * (chips - 1) + d - 1
        return send(chip_map.at[g], cross.at[g, other], cross_send.at[at], cross_recv.at[at], beside(other))

    def hop(g):
        return send(goes.at[g], came.at[g], chain_send.at[g], chain_recv.at[g], (after, place_in))

    def down(g, d):
        other, at = turned(d), g * (chips - 1) + d - 1
        return send(start.at[g, other], chip_start.at[chip * groups + g], down_send.at[at], down_recv.at[at], beside(other))

    def down_in(g, d):
        other, at = turned(chips - d), g * (chips - 1) + d - 1
        return send(start.at[g, other], chip_start.at[other * groups + g], down_send.at[at], down_recv.at[at], beside(other))

    def aside(src, m):
        return send(src.at[m], side.at[m], side_send.at[m], side_recv.at[m], sibling)

    @pl.when(stage == 0)
    def _():
        came[...] = jnp.zeros_like(came)

    def masks():
        return [lax.broadcasted_iota(jnp.int32, (SPAN, SPAN), axis) for axis in (0, 1)]

    row, lane = masks()
    for c in range(BASE - 1):
        pick[:, c * SPAN : (c + 1) * SPAN] = jnp.where(row == lane // BASE * BASE + c, 1.0, 0.0).astype(BF16)

    def group(g):
        ms = [c * groups + g for c in range(chips)]
        return ms, [core * owned + m for m in ms], [(1 - core) * owned + m for m in ms]

    def prepare(g):
        ms, mine, theirs = group(g)
        hs = mine + theirs
        a, b, wu, krow = block_map(*([ref[h] for h in hs] for ref in (k_ref, v_ref, b_ref)), *masks(), pick)
        for j, h in enumerate(hs):
            solved[h] = wu[j]
            norms[h] = krow[j]
        for j, m in enumerate(ms):
            outgoing[m, :SPAN] = a[chips + j]
            outgoing[m, SPAN:] = b[chips + j]
        for m in ms:
            give(m).start()
        for j, m in enumerate(ms):
            pair[m, core, :SPAN] = a[j]
            pair[m, core, SPAN:] = b[j]

    def compose(g):
        ms, _, _ = group(g)
        for m in ms:
            send(outgoing.at[m], pair.at[m, 1 - core], ab_send.at[m], ab_recv.at[m], sibling).wait_recv()
        early = [halves(jnp.concatenate([pair[m, 0, :SPAN], pair[m, 0, SPAN:]], 1)) for m in ms]
        late = [halves(pair[m, 1, :SPAN]) for m in ms]
        both = [dot_halves(x, y) for x, y in zip(late, early)]
        for j, m in enumerate(ms):
            chip_map[m, :SPAN] = both[j][:, :SPAN]
            chip_map[m, SPAN:] = both[j][:, SPAN:] + pair[m, 1, SPAN:]
        for d in range(1, chips):
            across(g, d).start()
        for j, m in enumerate(ms):
            first[m] = jnp.concatenate([x[:, :SPAN] for x in early[j]], 1)
        cross[g, chip] = chip_map[chip * groups + g]

    def compose_chips(g):
        for d in range(1, chips):
            across_in(g, d).wait_recv()
        both = jnp.concatenate([cross[g, 0, :SPAN], cross[g, 0, SPAN:]], 1)
        for c in range(1, chips):
            split = halves(both)
            if c == 1:
                inside[g, 0] = jnp.concatenate([x[:, :SPAN] for x in split], 1)
            late = halves(cross[g, c, :SPAN])
            if c < chips - 1:
                inside[g, c] = jnp.concatenate(late, 1)
            moved = dot_halves(late, split)
            both = jnp.concatenate([moved[:, :SPAN], moved[:, SPAN:] + cross[g, c, SPAN:]], 1)
        whole[g] = jnp.concatenate(halves(both[:, :SPAN]), 1)
        jump[g] = both[:, SPAN:]

    def apply(linear, state, constant):
        high, low = halves(state)
        return constant + dot(linear, jnp.concatenate([high, high], 0)) + dot(linear[:, :SPAN], low)

    def pass_on(g):
        @pl.when(stage > 0)
        def _():
            hop(g).wait_recv()

        @pl.when(stage < outer - 1)
        def _():
            goes[g] = apply(whole[g], came[g], jump[g])
            hop(g).start()

    def descend(g):
        state = came[g]
        for c in range(chips):
            start[g, c] = state
            if c < chips - 1:
                state = apply(inside[g, c], state, cross[g, c, SPAN:])
        for d in range(1, chips):
            down(g, d).start()
        chip_start[chip * groups + g] = start[g, chip]

    def spread(g):
        ms, _, _ = group(g)
        for d in range(1, chips):
            down_in(g, d).wait_recv()

        @pl.when(core == 1)
        def _():
            for m in ms:
                aside(chip_start, m).start()

        for m in ms:
            middle[m] = apply(first[m], chip_start[m], pair[m, 0, SPAN:])

        @pl.when(core == 0)
        def _():
            for m in ms:
                aside(middle, m).start()

    def read_terms(g):
        _, mine, theirs = group(g)
        hs = mine + theirs
        p, o = block_reads(*([ref[h] for h in hs] for ref in (q_ref, k_ref, solved, norms)), *masks())
        for j, h in enumerate(hs):
            solved[h] = jnp.concatenate([p[j], o[j]], 1)

    def put(hs, states):
        terms = [solved[h] for h in hs]
        states = [halves(x) for x in states]
        mixed = [x[:, SPAN:] + dot_halves(halves(x[:, :SPAN]), y) for x, y in zip(terms, states)]
        for h, x in zip(hs, mixed):
            o_ref[h] = x.astype(BF16)

    def finish(g):
        ms, mine, theirs = group(g)
        put(mine, [jnp.where(core == 0, chip_start[m], middle[m]) for m in ms])
        for m in ms:
            aside(middle, m).wait_recv()
        put(theirs, [side[m] for m in ms])

    ahead = jnp.maximum(4, jnp.minimum(groups, 4 + stage))
    busy = stage < 5 * outer // 8
    late = jnp.where(stage < outer // 4, groups + ahead, jnp.where(busy, groups, 0))
    below_at = jnp.maximum(late, ahead)

    def step(i, carry):
        def at(delay, do):
            @pl.when((i >= delay) & (i < delay + groups))
            def _():
                do(i - delay)

        at(0, prepare)
        at(2, compose)
        at(4, compose_chips)
        at(ahead, pass_on)
        at(late, read_terms)
        at(below_at, descend)
        at(below_at + 1, spread)
        at(below_at + 2, finish)
        return carry

    lax.fori_loop(0, groups + below_at + 2, step, 0)

    def drain(m, carry):
        give(m).wait_send()
        aside(middle, m).wait_send()
        return carry

    lax.fori_loop(0, owned, drain, 0)

    def drain_chain(g, carry):
        for d in range(1, chips):
            across(g, d).wait_send()
            down(g, d).wait_send()

        @pl.when(stage < outer - 1)
        def _():
            hop(g).wait_send()

        return carry

    lax.fori_loop(0, groups, drain_chain, 0)


def shards(outer, inner, query, keys, value, beta):
    tokens, heads, width = query.shape
    major = [jnp.transpose(x, (1, 0, 2)) for x in (query, keys, value)]
    gates = jnp.transpose(beta.astype(F32), (1, 0)).reshape(heads, 1, tokens)
    half, chips = heads // 2, inner // 2
    groups = half // chips
    vmem = pl.BlockSpec(memory_space=pltpu.VMEM)
    mixed = pl.pallas_call(
        functools.partial(kernel, outer, inner),
        out_shape=jax.ShapeDtypeStruct((heads, tokens, width), BF16),
        in_specs=[vmem] * 4,
        out_specs=vmem,
        scratch_shapes=[
            pltpu.VMEM((half, 2, 2 * width, width), F32),
            pltpu.VMEM((half, 2 * width, width), F32),
            pltpu.VMEM((heads, tokens, 2 * width), F32),
            pltpu.VMEM((heads, 1, tokens), F32),
            pltpu.VMEM((half, width, 2 * width), BF16),
            pltpu.VMEM((half, 2 * width, width), F32),
            pltpu.VMEM((groups, chips, 2 * width, width), F32),
            pltpu.VMEM((groups, width, 2 * width), BF16),
            pltpu.VMEM((groups, width, width), F32),
            pltpu.VMEM((groups, chips - 1, width, 2 * width), BF16),
            pltpu.VMEM((groups, width, width), F32),
            pltpu.VMEM((groups, width, width), F32),
            pltpu.VMEM((groups, chips, width, width), F32),
            *[pltpu.VMEM((half, width, width), F32)] * 3,
            pltpu.VMEM((SPAN, (BASE - 1) * SPAN), BF16),
            *[pltpu.SemaphoreType.DMA((half,))] * 4,
            *[pltpu.SemaphoreType.DMA((groups * (chips - 1),))] * 4,
            *[pltpu.SemaphoreType.DMA((groups,))] * 2,
        ],
        compiler_params=pltpu.CompilerParams(
            collective_id=0, has_side_effects=True, vmem_limit_bytes=40 * 2**20
        ),
        cost_estimate=pl.CostEstimate(flops=heads * 60 * 2 * 128**3, bytes_accessed=2**22, transcendentals=0),
    )(*major, gates)
    return jnp.transpose(mixed, (1, 0, 2))


def solution(mesh):
    placed = P(("outer", "inner"), None, None)
    return jax.shard_map(
        functools.partial(shards, mesh.shape["outer"], mesh.shape["inner"]),
        mesh=mesh,
        in_specs=(placed, placed, placed, P(("outer", "inner"), None)),
        out_specs=placed,
        check_vma=False,
    )
```
